32 devices in a mesh: ens: 2 (over x), lat: 4 (over y, core), lon: 4 (over z).
Axes of the slice: x: 2, y: 2, z: 4, core: 2. Of those that a mesh axis runs over, the one named last changes fastest.
Arguments:
- members_in: bfloat16 [8, 32, 64, 256], P('ens', 'lat', 'lon'), may hold values from -6 to 6
- out_grad: bfloat16 [8, 32, 64, 256], P('ens', 'lat', 'lon'), may hold values from -6 to 6
- weight: bfloat16 [9, 256, 256], replicated, may hold values from -0.125 to 0.125
- basis_blocks: float32 [8, 9, 3, 9], replicated, may hold values from -1.75 to 1.75
- cycle_block: int32 [32], replicated, may hold values from 0 to 7
- half_width: int32 [32, 3], replicated, may hold values from 1 to 4
Outputs:
- result: bfloat16 [8, 32, 64, 256], P('ens', 'lat', 'lon')
- in_grad: bfloat16 [8, 32, 64, 256], P('ens', 'lat', 'lon')
- weight_grad: float32 [9, 256, 256], P(None, 'lon')
The draws below stay inside these ranges and needn't reach their ends.
All inputs are finite; a program needn't handle non-finite values.
Results may differ from the reference program's by a relative error of at most 0.015.
Values may be sent and summed in bfloat16 or wider, within the bound.
A program may use at most 64 MiB of HBM per device.

```python
import math
import jax
import jax.numpy as jnp
from jax import lax

C = 256
K = 9
R = 1
H = 4
NB = 8
MEMBERS = 8
NLAT = 32
NLON = 64


def draw_cycle_block(key, part):
    cycle_ids = jax.random.randint(jax.random.fold_in(key, 11), (NLAT,), 0, NB)
    order_ids = jax.random.permutation(jax.random.fold_in(key, 12), NB).astype(jnp.int32)
    return cycle_ids.astype(jnp.int32).at[:NB].set(order_ids)


def draw_half_width(key, part):
    cycle_ids = jnp.arange(NLAT, dtype=jnp.int32)
    distance = jnp.minimum(cycle_ids, NLAT - 1 - cycle_ids)
    spread = max(NLAT // 2, 1)
    baseline = H - 2 * distance * H // spread
    jitter = jax.random.randint(jax.random.fold_in(key, 21), (NLAT, 2 * R + 1), 0, 2)
    widths = jnp.clip(baseline[:, None] + jitter, 1, H)
    widths = widths.at[0].set(H).at[NLAT - 1].set(H).at[NLAT // 2].set(1)
    return widths.astype(jnp.int32)


def levels(stream_key, extent, split, least, high):
    def one(dim, blocks):
        steps = jax.random.uniform(jax.random.fold_in(jax.random.fold_in(stream_key, 6), dim), (blocks,), jnp.float32, least / len(split), high / len(split))
        return jnp.repeat(jnp.exp(steps), extent[dim] // blocks).reshape((-1,) + (1,) * (len(extent) - dim - 1))

    loudness = one(*split[0])
    for cut in split[1:]:
        loudness = loudness * one(*cut)
    return loudness


def scatter_about(stream_key, shape, scale, reach, split=(), held_as=jnp.bfloat16):
    drawn = scale * jax.random.normal(stream_key, shape, jnp.float32)
    if split:
        drawn = drawn * levels(stream_key, shape, split, -0.22, 0.18)
    return jnp.clip(drawn, -reach, reach).astype(held_as)


def setup_inputs(seed: int = 0) -> dict:
    splits = jax.random.split(jax.random.key(seed), 7)
    members_in = scatter_about(splits[0], (MEMBERS, NLAT, NLON, C), 1.0, 6.0, ((0, 2), (1, 4), (2, 4)))
    out_grad = scatter_about(splits[1], (MEMBERS, NLAT, NLON, C), 1.0, 6.0, ((0, 2), (1, 4), (2, 4)))
    weight = scatter_about(splits[2], (K, C, C), (K * C) ** -0.5, 0.125)
    basis_blocks = scatter_about(splits[3], (NB, K, 2 * R + 1, 2 * H + 1), ((2 * R + 1) * H) ** -0.5, 1.75, (), jnp.float32)
    cycle_block = draw_cycle_block(jax.random.fold_in(splits[6], 71), 0)
    half_width = draw_half_width(jax.random.fold_in(splits[6], 71), 0)
    return dict(members_in=members_in, out_grad=out_grad, weight=weight, basis_blocks=basis_blocks, cycle_block=cycle_block, half_width=half_width)


def filter_table(basis_blocks, cycle_block, half_width):
    picked = basis_blocks[cycle_block]
    offsets = jnp.arange(2 * H + 1, dtype=jnp.int32) - H
    inside = jnp.abs(offsets)[None, None, :] <= half_width[:, :, None]
    return jnp.where(inside[:, None, :, :], picked, jnp.float32(0.0))

def stencil(values, coefficients):
    padded = jnp.pad(values, ((R, R), (0, 0), (0, 0)))
    summed = jnp.zeros((NLAT, NLON, K, C), jnp.float32)
    for offset_row in range(2 * R + 1):
        strip_rows = padded[offset_row:offset_row + NLAT].astype(jnp.float32)
        for offset_col in range(2 * H + 1):
            rolled = jnp.roll(strip_rows, H - offset_col, axis=1)
            summed = summed + coefficients[:, None, :, offset_row, offset_col, None] * rolled[:, :, None, :]
    return summed.astype(jnp.bfloat16)

def adjoint(values, coefficients):
    padded = jnp.pad(values, ((R, R), (0, 0), (0, 0)))
    wide_table = jnp.pad(coefficients, ((R, R), (0, 0), (0, 0), (0, 0)), mode='edge')
    summed = jnp.zeros((NLAT, NLON, K, C), jnp.float32)
    for offset_row in range(2 * R + 1):
        lead_row = 2 * R - offset_row
        strip_rows = padded[lead_row:lead_row + NLAT].astype(jnp.float32)
        rows_coef = wide_table[lead_row:lead_row + NLAT]
        for offset_col in range(2 * H + 1):
            rolled = jnp.roll(strip_rows, offset_col - H, axis=1)
            summed = summed + rows_coef[:, None, :, offset_row, offset_col, None] * rolled[:, :, None, :]
    return summed.astype(jnp.bfloat16)

def reference(members_in, out_grad, weight, basis_blocks, cycle_block, half_width):
    coefficients = filter_table(basis_blocks, cycle_block, half_width)
    flat_weight = weight.reshape(K * C, C)

    def single(running, member_pair):
        values, cotangent = member_pair
        features = stencil(values, coefficients)
        feature_rows = features.reshape(NLAT * NLON, K * C)
        mixed = jnp.dot(feature_rows, flat_weight, preferred_element_type=jnp.float32)
        activated, slope_fn = jax.vjp(jax.nn.gelu, mixed)
        cot_rows = cotangent.reshape(NLAT * NLON, C).astype(jnp.float32)
        output_rows = (values.reshape(NLAT * NLON, C).astype(jnp.float32) + activated).astype(jnp.bfloat16)
        grad_mixed = slope_fn(cot_rows)[0].astype(jnp.bfloat16)
        running = running + lax.dot_general(feature_rows, grad_mixed, (((0,), (0,)), ((), ())), preferred_element_type=jnp.float32)
        back = adjoint(grad_mixed.reshape(NLAT, NLON, C), coefficients)
        branch_rows = lax.dot_general(back.reshape(NLAT * NLON, K, C), weight, (((1, 2), (0, 2)), ((), ())), preferred_element_type=jnp.float32)
        grad_rows = (cot_rows + branch_rows).astype(jnp.bfloat16)
        return (running, (output_rows.reshape(NLAT, NLON, C), grad_rows.reshape(NLAT, NLON, C)))
    summed, (result, in_grad) = lax.scan(single, jnp.zeros((K * C, C), jnp.float32), (members_in, out_grad))
    weight_grad = (summed * (1.0 / math.sqrt(MEMBERS * NLAT * NLON))).reshape(K, C, C)
    return (result, in_grad, weight_grad)
```

```python
import functools
import math

import jax
import jax.numpy as jnp
import numpy as np
from jax import lax
from jax.experimental import pallas as pl
from jax.experimental.pallas import tpu as pltpu
from jax.sharding import PartitionSpec as P

R = 1
H = 4
MESH = pl.DeviceIdType.MESH
BF = jnp.bfloat16
F32 = jnp.float32


def layout(members, rows, cols):
    cells = [(i, j) for i in range(rows) for j in range(cols)]
    cells += [(-1, j) for j in range(cols)] + [(rows, j) for j in range(cols)]
    cells += [(i, j - H) for i in range(rows) for j in range(H)]
    cells += [(i, cols + j) for i in range(rows) for j in range(H)]
    for i in (-1, rows):
        for first in (-H, cols):
            cells += [(i, first + j) for j in range(H)]
    depth = -(-len(cells) // 128) * 128
    pos = np.full((8, depth), -1000, np.int32)
    for p, (i, j) in enumerate(cells):
        pos[0, p], pos[1, p] = i, j
    own = rows * cols
    index = lambda m, i, j: m * own + i * cols + j
    picks = [index(m, i, j) for m in range(members) for i in range(rows) for j in range(H)]
    picks += [
        index(m, i, cols - H + j) for m in range(members) for i in range(rows) for j in range(H)
    ]
    for i in (0, rows - 1):
        for first in (0, cols - H):
            picks += [index(m, i, first + j) for m in range(members) for j in range(H)]
    select = np.zeros((len(picks), members * own), np.float32)
    select[np.arange(len(picks)), picks] = 1
    corners = 4 * members * H
    regroup = np.zeros((corners, corners), np.float32)
    for m in range(members):
        for q in range(4):
            for j in range(H):
                regroup[(m * 4 + q) * H + j, (q * members + m) * H + j] = 1
    return len(cells), depth, pos, select, regroup


def block_kernel(
    dims,
    x_hbm, og_hbm, w_hbm, basis_ref, cb_ref, hw_ref, pos_ref, reach_ref, select_ref, regroup_ref,
    res_hbm, ing_hbm, wg_hbm,
    xp, gp, og, w, feats, fwd, adj, packs, crecv, res, ing, wg, lsem, ssem, rsem,
):
    members, rows, cols, chan, basis, used, depth, lats, lons, total, scale = dims
    own = rows * cols
    rim = rows * H
    taps = 2 * H + 1
    lat = lax.axis_index("lat")
    lon = lax.axis_index("lon")
    west = lax.rem(lon + lons - 1, lons)
    east = lax.rem(lon + 1, lons)
    has_n = lat > 0
    has_s = lat < lats - 1

    load_x = pltpu.make_async_copy(x_hbm, xp.at[:, pl.ds(0, own), :], lsem.at[0])
    load_x.start()
    load_og = pltpu.make_async_copy(og_hbm, og, lsem.at[1])
    load_og.start()
    load_w = pltpu.make_async_copy(w_hbm, w, lsem.at[2])
    load_w.start()

    barrier = pltpu.get_barrier_semaphore()

    def greet(where):
        pl.semaphore_signal(barrier, inc=1, device_id=where, device_id_type=MESH)

    greet({"lon": west})
    greet({"lon": east})

    @pl.when(has_n)
    def _():
        for z in (lon, west, east):
            greet({"lat": lat - 1, "lon": z})

    @pl.when(has_s)
    def _():
        for z in (lon, west, east):
            greet({"lat": lat + 1, "lon": z})

    def clear(pad, land):
        pad[:, used:, :] = jnp.zeros((members, depth - used, chan), BF)

        @pl.when(jnp.logical_not(has_n))
        def _():
            pad[:, own : own + cols, :] = jnp.zeros((members, cols, chan), BF)
            land[0:2] = jnp.zeros((2,) + land.shape[1:], BF)

        @pl.when(jnp.logical_not(has_s))
        def _():
            pad[:, own + cols : own + 2 * cols, :] = jnp.zeros((members, cols, chan), BF)
            land[2:4] = jnp.zeros((2,) + land.shape[1:], BF)

    wide = members * rim
    mh = members * H

    def copies(t):
        pad = (xp, gp)[t]
        pack = packs.at[t]
        land = crecv.at[t]
        top, bottom = pl.ds(own, cols), pl.ds(own + cols, cols)
        left, right = pl.ds(own + 2 * cols, rim), pl.ds(own + 2 * cols + rim, rim)
        corner = lambda q: pack.at[pl.ds(2 * wide + q * mh, mh)]
        north, south = {"lat": lat - 1}, {"lat": lat + 1}
        plan = [
            (pad.at[:, pl.ds(0, cols), :], pad.at[:, bottom, :], north),
            (pad.at[:, pl.ds(own - cols, cols), :], pad.at[:, top, :], south),
            (None, right, {"lon": west}),
            (None, left, {"lon": east}),
            (corner(0), land.at[3], {"lat": lat - 1, "lon": west}),
            (corner(1), land.at[2], {"lat": lat - 1, "lon": east}),
            (corner(2), land.at[1], {"lat": lat + 1, "lon": west}),
            (corner(3), land.at[0], {"lat": lat + 1, "lon": east}),
        ]
        out = {}
        slot = 0
        for q, (src, dst, where) in enumerate(plan):
            if src is None:
                parts = [
                    (pack.at[pl.ds((q - 2) * wide + m * rim, rim)], pad.at[m, dst, :])
                    for m in range(members)
                ]
            else:
                parts = [(src, dst)]
            out[q] = []
            for a, b in parts:
                out[q].append(
                    pltpu.make_async_remote_copy(
                        src_ref=a, dst_ref=b, send_sem=ssem.at[t, slot], recv_sem=rsem.at[t, slot],
                        device_id=where, device_id_type=MESH,
                    )
                )
                slot += 1
        return out

    NORTH, SOUTH, SIDES = (0, 4, 5), (1, 6, 7), (2, 3)

    def each(c, qs, act):
        for q in qs:
            for one in c[q]:
                act(one)

    def send(t):
        c = copies(t)
        pad = (xp, gp)[t]

        flat = pad[:, :own, :].reshape(members * own, chan)
        packs[t] = jnp.dot(select_ref[...], flat, preferred_element_type=F32).astype(BF)
        each(c, SIDES, lambda one: one.start())

        @pl.when(has_n)
        def _():
            each(c, NORTH, lambda one: one.start())

        @pl.when(has_s)
        def _():
            each(c, SOUTH, lambda one: one.start())

    def receive(t):
        c = copies(t)
        pad = (xp, gp)[t]

        each(c, SIDES, lambda one: one.wait_recv())

        @pl.when(has_s)
        def _():
            each(c, NORTH, lambda one: one.wait_recv())

        @pl.when(has_n)
        def _():
            each(c, SOUTH, lambda one: one.wait_recv())

        got = jnp.dot(
            regroup_ref[...], crecv[t].reshape(4 * mh, chan), preferred_element_type=F32
        ).astype(BF)
        for m in range(members):
            pad[m, used - 4 * H : used, :] = got[m * 4 * H : (m + 1) * 4 * H]

    def sent(t):
        c = copies(t)
        each(c, SIDES, lambda one: one.wait_send())

        @pl.when(has_n)
        def _():
            each(c, NORTH, lambda one: one.wait_send())

        @pl.when(has_s)
        def _():
            each(c, SOUTH, lambda one: one.wait_send())

    clear(xp, crecv.at[0])
    clear(gp, crecv.at[1])
    load_x.wait()
    pl.semaphore_wait(
        barrier, 2 + 3 * has_n.astype(jnp.int32) + 3 * has_s.astype(jnp.int32)
    )
    send(0)

    lane = lax.broadcasted_iota(jnp.int32, reach_ref.shape, 1)
    first = lat * rows
    cell_i, cell_j = pos_ref[0:1, :], pos_ref[1:2, :]
    step = lax.broadcasted_iota(jnp.int32, (128, depth), 0)
    col = lax.broadcasted_iota(jnp.int32, (cols, depth), 0)
    ahead = cell_j - col + H
    behind = col - cell_j + H

    def filters(i):
        cyc = jnp.clip(first + i, 0, total - 1)
        table = basis_ref[cb_ref[cyc]]
        span = jnp.where(
            lane == 0, hw_ref[cyc, 0], jnp.where(lane == 1, hw_ref[cyc, 1], hw_ref[cyc, 2])
        )
        return jnp.where(reach_ref[...] <= span, table, 0.0)

    def expand(table, rowsel, offset, dst, i):
        spread = jnp.dot(table.astype(BF), rowsel.astype(BF), preferred_element_type=F32)
        for k in range(basis):
            acc = jnp.zeros((cols, depth), F32)
            for d in range(taps):
                line = spread[k * taps + d : k * taps + d + 1, :]
                acc = jnp.where(offset == d, line, acc)
            dst[pl.ds(pl.multiple_of(k * own + i * cols, cols), cols), :] = acc.astype(BF)

    def build(i, carry):
        here = filters(i)
        onward = jnp.where(cell_i - i + R == step, 1.0, 0.0)
        expand(here, onward, ahead, fwd, i)
        table = jnp.where(
            lane == 0, filters(i + 1), jnp.where(lane == 1, here, filters(i - 1))
        )
        back = jnp.where(i + R - cell_i == step, 1.0, 0.0)
        expand(jnp.where(lane < 3, table, 0.0), back, behind, adj, i)
        return carry

    lax.fori_loop(0, rows, build, 0)

    def spread_all(mat, pad):
        def one(m, carry):
            block = pad[m]
            at = pl.ds(pl.multiple_of(m * own, own), own)
            for k in range(basis):
                feats[at, k * chan : (k + 1) * chan] = jnp.dot(
                    mat[k * own : (k + 1) * own, :], block, preferred_element_type=F32
                ).astype(BF)
            return carry

        lax.fori_loop(0, members, one, 0)

    receive(0)
    spread_all(fwd, xp)
    load_w.wait()
    load_og.wait()

    def forward(m, carry):
        at = pl.ds(pl.multiple_of(m * own, own), own)
        v = jnp.dot(
            feats[at, :], w[...].reshape(basis * chan, chan), preferred_element_type=F32
        )
        root = math.sqrt(2.0 / math.pi)
        vv = v * v
        th = jnp.tanh(root * (v + 0.044715 * (vv * v)))
        half = 0.5 * (1.0 + th)
        res[m] = (xp[m, :own, :].astype(F32) + v * half).astype(BF)
        slope = half + 0.5 * v * (1.0 - th * th) * (root * (1.0 + 3 * 0.044715 * vv))
        gp[m, :own, :] = (og[m].astype(F32) * slope).astype(BF)
        return carry

    lax.fori_loop(0, members, forward, 0)
    send(1)
    save_res = pltpu.make_async_copy(res, res_hbm, lsem.at[3])
    save_res.start()

    grad = gp[:, :own, :].reshape(members * own, chan)
    for k in range(basis):
        part = lax.dot_general(
            feats[:, k * chan : (k + 1) * chan], grad, (((0,), (0,)), ((), ())),
            preferred_element_type=F32,
        )
        wg[k] = (part * scale).astype(BF)
    save_wg = pltpu.make_async_copy(wg, wg_hbm, lsem.at[4])
    save_wg.start()

    receive(1)
    spread_all(adj, gp)

    def backward(m, carry):
        at = pl.ds(pl.multiple_of(m * own, own), own)
        acc = og[m].astype(F32)
        for k in range(basis):
            acc = acc + lax.dot_general(
                feats[at, k * chan : (k + 1) * chan], w[k], (((1,), (1,)), ((), ())),
                preferred_element_type=F32,
            )
        ing[m] = acc.astype(BF)
        return carry

    lax.fori_loop(0, members, backward, 0)
    save_ing = pltpu.make_async_copy(ing, ing_hbm, lsem.at[5])
    save_ing.start()
    sent(0)
    sent(1)
    save_res.wait()
    save_wg.wait()
    save_ing.wait()


def shards(members_in, out_grad, weight, basis_blocks, cycle_block, half_width):
    members, rows, cols, chan = members_in.shape
    blocks, basis, reach, taps = basis_blocks.shape
    own = rows * cols
    lats, lons = lax.axis_size("lat"), lax.axis_size("lon")
    used, depth, pos, select, regroup = layout(members, rows, cols)
    lines = -(-basis * taps // 16) * 16
    table = jnp.transpose(basis_blocks, (0, 1, 3, 2)).reshape(blocks, basis * taps, reach)
    table = jnp.pad(table, ((0, 0), (0, lines - basis * taps), (0, 128 - reach)))
    far = np.broadcast_to(np.abs(np.arange(lines) % taps - H)[:, None], (lines, 128))
    cell_count = members * lax.axis_size("ens") * own * lats * lons
    dims = (
        members, rows, cols, chan, basis, used, depth, lats, lons, cycle_block.shape[0],
        1.0 / math.sqrt(cell_count),
    )
    anywhere = pl.BlockSpec(memory_space=pl.ANY)
    vmem = pl.BlockSpec(memory_space=pltpu.VMEM)
    smem = pl.BlockSpec(memory_space=pltpu.SMEM)
    cells = (members, own, chan)
    padded = (members, depth, chan)
    slots = 6 + 2 * members
    res, ing, local_grad = pl.pallas_call(
        functools.partial(block_kernel, dims),
        out_shape=[
            jax.ShapeDtypeStruct(cells, BF),
            jax.ShapeDtypeStruct(cells, BF),
            jax.ShapeDtypeStruct((basis, chan, chan), BF),
        ],
        in_specs=[anywhere] * 3 + [vmem, smem, smem] + [vmem] * 4,
        out_specs=[anywhere] * 3,
        scratch_shapes=[
            pltpu.VMEM(padded, BF),
            pltpu.VMEM(padded, BF),
            pltpu.VMEM(cells, BF),
            pltpu.VMEM((basis, chan, chan), BF),
            pltpu.VMEM((members * own, basis * chan), BF),
            pltpu.VMEM((basis * own, depth), BF),
            pltpu.VMEM((basis * own, depth), BF),
            pltpu.VMEM((2, select.shape[0], chan), BF),
            pltpu.VMEM((2, 4, members * H, chan), BF),
            pltpu.VMEM(cells, BF),
            pltpu.VMEM(cells, BF),
            pltpu.VMEM((basis, chan, chan), BF),
            pltpu.SemaphoreType.DMA((6,)),
            pltpu.SemaphoreType.DMA((2, slots)),
            pltpu.SemaphoreType.DMA((2, slots)),
        ],
        compiler_params=pltpu.CompilerParams(
            collective_id=0, has_side_effects=True, vmem_limit_bytes=48 * 1024 * 1024
        ),
    )(
        members_in.reshape(cells), out_grad.reshape(cells), weight, table, cycle_block, half_width,
        jnp.asarray(pos), jnp.asarray(far, dtype=jnp.int32), jnp.asarray(select, dtype=BF),
        jnp.asarray(regroup, dtype=BF),
    )
    share = lax.psum_scatter(local_grad, "lon", scatter_dimension=1, tiled=True)
    weight_grad = lax.psum(share, ("ens", "lat")).astype(F32)
    return (res.reshape(members_in.shape), ing.reshape(members_in.shape), weight_grad)


def solution(mesh):
    cells = P("ens", "lat", "lon", None)
    return jax.shard_map(
        shards,
        mesh=mesh,
        in_specs=(cells, cells, P(), P(), P(), P()),
        out_specs=(cells, cells, P(None, "lon", None)),
        check_vma=False,
    )
```

```python
import functools
import math

import jax
import jax.numpy as jnp
import numpy as np
from jax import lax
from jax.experimental import pallas as pl
from jax.experimental.pallas import tpu as pltpu
from jax.sharding import PartitionSpec as P

R = 1
H = 4
MESH = pl.DeviceIdType.MESH
BF = jnp.bfloat16
F32 = jnp.float32


def layout(members, rows, cols):
    cells = [(i, j) for i in range(rows) for j in range(cols)]
    cells += [(-1, j) for j in range(cols)] + [(rows, j) for j in range(cols)]
    cells += [(i, j - H) for i in range(rows) for j in range(H)]
    cells += [(i, cols + j) for i in range(rows) for j in range(H)]
    for i in (-1, rows):
        for first in (-H, cols):
            cells += [(i, first + j) for j in range(H)]
    depth = -(-len(cells) // 128) * 128
    pos = np.full((8, depth), -1000, np.int32)
    for p, (i, j) in enumerate(cells):
        pos[0, p], pos[1, p] = i, j
    own = rows * cols
    index = lambda m, i, j: m * own + i * cols + j
    picks = [index(m, i, j) for m in range(members) for i in range(rows) for j in range(H)]
    picks += [
        index(m, i, cols - H + j) for m in range(members) for i in range(rows) for j in range(H)
    ]
    for i in (0, rows - 1):
        for first in (0, cols - H):
            picks += [index(m, i, first + j) for m in range(members) for j in range(H)]
    select = np.zeros((len(picks), members * own), np.float32)
    select[np.arange(len(picks)), picks] = 1
    corners = 4 * members * H
    regroup = np.zeros((corners, corners), np.float32)
    for m in range(members):
        for q in range(4):
            for j in range(H):
                regroup[(m * 4 + q) * H + j, (q * members + m) * H + j] = 1
    return len(cells), depth, pos, select, regroup


def block_kernel(
    dims,
    x_hbm, og_hbm, w_hbm, basis_ref, cb_ref, hw_ref, pos_ref, reach_ref, select_ref, regroup_ref,
    res_hbm, ing_hbm, wg_hbm,
    xp, gp, og, w, feats, fwd, adj, packs, crecv, res, ing, wg, pair_in, plane_in, plane_sum,
    lon_in, done, share, lsem, ssem, rsem, wssem, wrsem,
):
    members, rows, cols, chan, basis, used, depth, enss, lats, lons, total, scale = dims
    own = rows * cols
    rim = rows * H
    taps = 2 * H + 1
    lat = lax.axis_index("lat")
    lon = lax.axis_index("lon")
    west = lax.rem(lon + lons - 1, lons)
    east = lax.rem(lon + 1, lons)
    has_n = lat > 0
    has_s = lat < lats - 1
    ens = lax.axis_index("ens")
    chips = lats // 2
    plane = enss * chips
    core = lax.rem(lat, 2)
    mine = ens * chips + lat // 2
    held = chan // lons
    piece = wg.shape[2] // plane
    half = chan // 2

    load_x = pltpu.make_async_copy(x_hbm, xp.at[:, pl.ds(0, own), :], lsem.at[0])
    load_x.start()
    load_og = pltpu.make_async_copy(og_hbm, og, lsem.at[1])
    load_og.start()
    load_w = pltpu.make_async_copy(w_hbm, w, lsem.at[2])
    load_w.start()

    barrier = pltpu.get_barrier_semaphore()

    def greet(where):
        pl.semaphore_signal(barrier, inc=1, device_id=where, device_id_type=MESH)

    greet({"lon": west})
    greet({"lon": east})

    def in_plane(step):
        other = lax.rem(mine + step, plane)
        return {"ens": other // chips, "lat": 2 * lax.rem(other, chips) + core}, other

    def in_group(step):
        other = lax.rem(ens * lats + lat + step, enss * lats)
        return {"ens": other // lats, "lat": lax.rem(other, lats)}

    for hop in range(1, enss * lats):
        greet(in_group(hop))
    for hop in range(1, lons):
        greet({"lon": lax.rem(lon + hop, lons)})

    @pl.when(has_n)
    def _():
        for z in (lon, west, east):
            greet({"lat": lat - 1, "lon": z})

    @pl.when(has_s)
    def _():
        for z in (lon, west, east):
            greet({"lat": lat + 1, "lon": z})

    def clear(pad, land):
        pad[:, used:, :] = jnp.zeros((members, depth - used, chan), BF)

        @pl.when(jnp.logical_not(has_n))
        def _():
            pad[:, own : own + cols, :] = jnp.zeros((members, cols, chan), BF)
            land[0:2] = jnp.zeros((2,) + land.shape[1:], BF)

        @pl.when(jnp.logical_not(has_s))
        def _():
            pad[:, own + cols : own + 2 * cols, :] = jnp.zeros((members, cols, chan), BF)
            land[2:4] = jnp.zeros((2,) + land.shape[1:], BF)

    wide = members * rim
    mh = members * H

    def copies(t):
        pad = (xp, gp)[t]
        pack = packs.at[t]
        land = crecv.at[t]
        top, bottom = pl.ds(own, cols), pl.ds(own + cols, cols)
        left, right = pl.ds(own + 2 * cols, rim), pl.ds(own + 2 * cols + rim, rim)
        corner = lambda q: pack.at[pl.ds(2 * wide + q * mh, mh)]
        north, south = {"lat": lat - 1}, {"lat": lat + 1}
        plan = [
            (pad.at[:, pl.ds(0, cols), :], pad.at[:, bottom, :], north),
            (pad.at[:, pl.ds(own - cols, cols), :], pad.at[:, top, :], south),
            (None, right, {"lon": west}),
            (None, left, {"lon": east}),
            (corner(0), land.at[3], {"lat": lat - 1, "lon": west}),
            (corner(1), land.at[2], {"lat": lat - 1, "lon": east}),
            (corner(2), land.at[1], {"lat": lat + 1, "lon": west}),
            (corner(3), land.at[0], {"lat": lat + 1, "lon": east}),
        ]
        out = {}
        slot = 0
        for q, (src, dst, where) in enumerate(plan):
            if src is None:
                parts = [
                    (pack.at[pl.ds((q - 2) * wide + m * rim, rim)], pad.at[m, dst, :])
                    for m in range(members)
                ]
            else:
                parts = [(src, dst)]
            out[q] = []
            for a, b in parts:
                out[q].append(
                    pltpu.make_async_remote_copy(
                        src_ref=a, dst_ref=b, send_sem=ssem.at[t, slot], recv_sem=rsem.at[t, slot],
                        device_id=where, device_id_type=MESH,
                    )
                )
                slot += 1
        return out

    NORTH, SOUTH, SIDES = (0, 4, 5), (1, 6, 7), (2, 3)

    def each(c, qs, act):
        for q in qs:
            for one in c[q]:
                act(one)

    def send(t):
        c = copies(t)
        pad = (xp, gp)[t]

        flat = pad[:, :own, :].reshape(members * own, chan)
        packs[t] = jnp.dot(select_ref[...], flat, preferred_element_type=F32).astype(BF)
        each(c, SIDES, lambda one: one.start())

        @pl.when(has_n)
        def _():
            each(c, NORTH, lambda one: one.start())

        @pl.when(has_s)
        def _():
            each(c, SOUTH, lambda one: one.start())

    def receive(t):
        c = copies(t)
        pad = (xp, gp)[t]

        each(c, SIDES, lambda one: one.wait_recv())

        @pl.when(has_s)
        def _():
            each(c, NORTH, lambda one: one.wait_recv())

        @pl.when(has_n)
        def _():
            each(c, SOUTH, lambda one: one.wait_recv())

        got = jnp.dot(
            regroup_ref[...], crecv[t].reshape(4 * mh, chan), preferred_element_type=F32
        ).astype(BF)
        for m in range(members):
            pad[m, used - 4 * H : used, :] = got[m * 4 * H : (m + 1) * 4 * H]

    def sent(t):
        c = copies(t)
        each(c, SIDES, lambda one: one.wait_send())

        @pl.when(has_n)
        def _():
            each(c, NORTH, lambda one: one.wait_send())

        @pl.when(has_s)
        def _():
            each(c, SOUTH, lambda one: one.wait_send())

    clear(xp, crecv.at[0])
    clear(gp, crecv.at[1])
    load_x.wait()
    pl.semaphore_wait(
        barrier,
        lons + enss * lats + 3 * has_n.astype(jnp.int32) + 3 * has_s.astype(jnp.int32),
    )
    send(0)

    lane = lax.broadcasted_iota(jnp.int32, reach_ref.shape, 1)
    first = lat * rows
    cell_i, cell_j = pos_ref[0:1, :], pos_ref[1:2, :]
    step = lax.broadcasted_iota(jnp.int32, (128, depth), 0)
    col = lax.broadcasted_iota(jnp.int32, (cols, depth), 0)
    ahead = cell_j - col + H
    behind = col - cell_j + H

    def filters(i):
        cyc = jnp.clip(first + i, 0, total - 1)
        table = basis_ref[cb_ref[cyc]]
        span = jnp.where(
            lane == 0, hw_ref[cyc, 0], jnp.where(lane == 1, hw_ref[cyc, 1], hw_ref[cyc, 2])
        )
        return jnp.where(reach_ref[...] <= span, table, 0.0)

    def expand(table, rowsel, offset, dst, i):
        spread = jnp.dot(table.astype(BF), rowsel.astype(BF), preferred_element_type=F32)
        for k in range(basis):
            acc = jnp.zeros((cols, depth), F32)
            for d in range(taps):
                line = spread[k * taps + d : k * taps + d + 1, :]
                acc = jnp.where(offset == d, line, acc)
            dst[pl.ds(pl.multiple_of(k * own + i * cols, cols), cols), :] = acc.astype(BF)

    def build(i, carry):
        here = filters(i)
        onward = jnp.where(cell_i - i + R == step, 1.0, 0.0)
        expand(here, onward, ahead, fwd, i)
        table = jnp.where(
            lane == 0, filters(i + 1), jnp.where(lane == 1, here, filters(i - 1))
        )
        back = jnp.where(i + R - cell_i == step, 1.0, 0.0)
        expand(jnp.where(lane < 3, table, 0.0), back, behind, adj, i)
        return carry

    lax.fori_loop(0, rows, build, 0)

    def spread_all(mat, pad):
        def one(m, carry):
            block = pad[m]
            at = pl.ds(pl.multiple_of(m * own, own), own)
            for k in range(basis):
                feats[at, k * chan : (k + 1) * chan] = jnp.dot(
                    mat[k * own : (k + 1) * own, :], block, preferred_element_type=F32
                ).astype(BF)
            return carry

        lax.fori_loop(0, members, one, 0)

    receive(0)
    spread_all(fwd, xp)
    load_w.wait()
    load_og.wait()

    def forward(m, carry):
        at = pl.ds(pl.multiple_of(m * own, own), own)
        v = jnp.dot(
            feats[at, :], w[...].reshape(basis * chan, chan), preferred_element_type=F32
        )
        root = math.sqrt(2.0 / math.pi)
        vv = v * v
        th = jnp.tanh(root * (v + 0.044715 * (vv * v)))
        half = 0.5 * (1.0 + th)
        res[m] = (xp[m, :own, :].astype(F32) + v * half).astype(BF)
        slope = half + 0.5 * v * (1.0 - th * th) * (root * (1.0 + 3 * 0.044715 * vv))
        gp[m, :own, :] = (og[m].astype(F32) * slope).astype(BF)
        return carry

    lax.fori_loop(0, members, forward, 0)
    send(1)
    save_res = pltpu.make_async_copy(res, res_hbm, lsem.at[3])
    save_res.start()

    grad = gp[:, :own, :].reshape(members * own, chan)
    for k in range(basis):
        part = lax.dot_general(
            feats[:, k * chan : (k + 1) * chan], grad, (((0,), (0,)), ((), ())),
            preferred_element_type=F32,
        )
        part = (part * scale).astype(wg.dtype)
        for z in range(lons):
            for h in range(2):
                wg[h, z, k * held : (k + 1) * held, :] = part[
                    z * held : (z + 1) * held, h * half : (h + 1) * half
                ]

    def push(src, dst, slot, where):
        one = pltpu.make_async_remote_copy(
            src_ref=src, dst_ref=dst, send_sem=wssem.at[slot], recv_sem=wrsem.at[slot],
            device_id=where, device_id_type=MESH,
        )
        one.start()
        return one

    pushed = [push(wg.at[1 - core], pair_in, 0, {"lat": lat + 1 - 2 * core})]
    receive(1)
    spread_all(adj, gp)

    pushed[0].wait_recv()

    def add_pair(z, carry):
        wg[core, z] = (wg[core, z].astype(F32) + pair_in[z].astype(F32)).astype(BF)
        return carry

    lax.fori_loop(0, lons, add_pair, 0)
    to_plane = []
    for hop in range(1, plane):
        where, other = in_plane(hop)
        at = pl.ds(pl.multiple_of(other * piece, 16), piece)
        to_plane.append(push(wg.at[core, :, at, :], plane_in.at[hop - 1], hop, where))

    def backward(m, carry):
        at = pl.ds(pl.multiple_of(m * own, own), own)
        acc = og[m].astype(F32)
        for k in range(basis):
            acc = acc + lax.dot_general(
                feats[at, k * chan : (k + 1) * chan], w[k], (((1,), (1,)), ((), ())),
                preferred_element_type=F32,
            )
        ing[m] = acc.astype(BF)
        return carry

    lax.fori_loop(0, members, backward, 0)
    save_ing = pltpu.make_async_copy(ing, ing_hbm, lsem.at[5])
    save_ing.start()
    sent(0)
    sent(1)
    save_res.wait()

    for one in to_plane:
        one.wait_recv()
    own_piece = pl.ds(pl.multiple_of(mine * piece, 16), piece)

    def add_plane(z, carry):
        acc = wg[core, z, own_piece, :].astype(F32)
        for hop in range(plane - 1):
            acc = acc + plane_in[hop, z].astype(F32)
        plane_sum[z] = acc.astype(BF)
        return carry

    lax.fori_loop(0, lons, add_plane, 0)
    along = []
    for hop in range(1, lons):
        other = lax.rem(lon + hop, lons)
        along.append(
            push(plane_sum.at[other], lon_in.at[hop - 1], plane - 1 + hop, {"lon": other})
        )
    for one in along:
        one.wait_recv()
    acc = plane_sum[lon].astype(F32)
    for hop in range(lons - 1):
        acc = acc + lon_in[hop].astype(F32)
    done[core, own_piece, :] = acc.astype(BF)
    spot = done.at[core, own_piece, :]
    around = [
        push(spot, spot, plane + lons - 2 + hop, in_group(hop)) for hop in range(1, enss * lats)
    ]
    for one in around:
        one.wait_recv()
    for h in range(2):
        full = done[h].astype(F32)
        for k in range(basis):
            share[k, :, h * half : (h + 1) * half] = full[k * held : (k + 1) * held]
    save_wg = pltpu.make_async_copy(share, wg_hbm, lsem.at[4])
    save_wg.start()
    for one in pushed + to_plane + along + around:
        one.wait_send()
    save_wg.wait()
    save_ing.wait()


def shards(members_in, out_grad, weight, basis_blocks, cycle_block, half_width):
    members, rows, cols, chan = members_in.shape
    blocks, basis, reach, taps = basis_blocks.shape
    own = rows * cols
    enss, lats, lons = (lax.axis_size(axis) for axis in ("ens", "lat", "lon"))
    plane = enss * lats // 2
    held = chan // lons
    span = -(-basis * held // (16 * plane)) * 16 * plane
    piece = span // plane
    half = chan // 2
    used, depth, pos, select, regroup = layout(members, rows, cols)
    lines = -(-basis * taps // 16) * 16
    table = jnp.transpose(basis_blocks, (0, 1, 3, 2)).reshape(blocks, basis * taps, reach)
    table = jnp.pad(table, ((0, 0), (0, lines - basis * taps), (0, 128 - reach)))
    far = np.broadcast_to(np.abs(np.arange(lines) % taps - H)[:, None], (lines, 128))
    cell_count = members * enss * own * lats * lons
    dims = (
        members, rows, cols, chan, basis, used, depth, enss, lats, lons, cycle_block.shape[0],
        1.0 / math.sqrt(cell_count),
    )
    anywhere = pl.BlockSpec(memory_space=pl.ANY)
    vmem = pl.BlockSpec(memory_space=pltpu.VMEM)
    smem = pl.BlockSpec(memory_space=pltpu.SMEM)
    cells = (members, own, chan)
    padded = (members, depth, chan)
    slots = 6 + 2 * members
    pushes = plane + lons - 1 + enss * lats - 1
    res, ing, weight_grad = pl.pallas_call(
        functools.partial(block_kernel, dims),
        out_shape=[
            jax.ShapeDtypeStruct(cells, BF),
            jax.ShapeDtypeStruct(cells, BF),
            jax.ShapeDtypeStruct((basis, held, chan), F32),
        ],
        in_specs=[anywhere] * 3 + [vmem, smem, smem] + [vmem] * 4,
        out_specs=[anywhere] * 3,
        scratch_shapes=[
            pltpu.VMEM(padded, BF),
            pltpu.VMEM(padded, BF),
            pltpu.VMEM(cells, BF),
            pltpu.VMEM((basis, chan, chan), BF),
            pltpu.VMEM((members * own, basis * chan), BF),
            pltpu.VMEM((basis * own, depth), BF),
            pltpu.VMEM((basis * own, depth), BF),
            pltpu.VMEM((2, select.shape[0], chan), BF),
            pltpu.VMEM((2, 4, members * H, chan), BF),
            pltpu.VMEM(cells, BF),
            pltpu.VMEM(cells, BF),
            pltpu.VMEM((2, lons, span, half), BF),
            pltpu.VMEM((lons, span, half), BF),
            pltpu.VMEM((plane - 1, lons, piece, half), BF),
            pltpu.VMEM((lons, piece, half), BF),
            pltpu.VMEM((lons - 1, piece, half), BF),
            pltpu.VMEM((2, span, half), BF),
            pltpu.VMEM((basis, held, chan), F32),
            pltpu.SemaphoreType.DMA((6,)),
            pltpu.SemaphoreType.DMA((2, slots)),
            pltpu.SemaphoreType.DMA((2, slots)),
            pltpu.SemaphoreType.DMA((pushes,)),
            pltpu.SemaphoreType.DMA((pushes,)),
        ],
        compiler_params=pltpu.CompilerParams(
            collective_id=0, has_side_effects=True, vmem_limit_bytes=48 * 1024 * 1024
        ),
    )(
        members_in.reshape(cells), out_grad.reshape(cells), weight, table, cycle_block, half_width,
        jnp.asarray(pos), jnp.asarray(far, dtype=jnp.int32), jnp.asarray(select, dtype=BF),
        jnp.asarray(regroup, dtype=BF),
    )
    return (res.reshape(members_in.shape), ing.reshape(members_in.shape), weight_grad)


def solution(mesh):
    cells = P("ens", "lat", "lon", None)
    return jax.shard_map(
        shards,
        mesh=mesh,
        in_specs=(cells, cells, P(), P(), P(), P()),
        out_specs=(cells, cells, P(None, "lon", None)),
        check_vma=False,
    )
```

```python
import functools
import math

import jax
import jax.numpy as jnp
import numpy as np
from jax import lax
from jax.experimental import pallas as pl
from jax.experimental.pallas import tpu as pltpu
from jax.sharding import PartitionSpec as P

R = 1
H = 4
MESH = pl.DeviceIdType.MESH
BF = jnp.bfloat16
F32 = jnp.float32


def layout(members, rows, cols):
    cells = [(i, j) for i in range(rows) for j in range(cols)]
    cells += [(-1, j) for j in range(cols)] + [(rows, j) for j in range(cols)]
    cells += [(i, j - H) for i in range(rows) for j in range(H)]
    cells += [(i, cols + j) for i in range(rows) for j in range(H)]
    for i in (-1, rows):
        for first in (-H, cols):
            cells += [(i, first + j) for j in range(H)]
    depth = -(-len(cells) // 128) * 128
    pos = np.full((8, depth), -1000, np.int32)
    for p, (i, j) in enumerate(cells):
        pos[0, p], pos[1, p] = i, j
    own = rows * cols
    picks = [i * cols + j for i in range(rows) for j in range(H)]
    picks += [i * cols + cols - H + j for i in range(rows) for j in range(H)]
    picks += [i * cols + f + j for i in (0, rows - 1) for f in (0, cols - H) for j in range(H)]
    select = np.zeros((len(picks), own), np.float32)
    select[np.arange(len(picks)), picks] = 1
    corners = 4 * members * H
    regroup = np.zeros((corners, corners), np.float32)
    for m in range(members):
        for q in range(4):
            for j in range(H):
                regroup[(m * 4 + q) * H + j, (q * members + m) * H + j] = 1
    return len(cells), depth, pos, select, regroup


def block_kernel(
    dims,
    x_hbm, og_hbm, w_hbm, basis_ref, cb_ref, hw_ref, pos_ref, select_ref, regroup_ref,
    res_hbm, ing_hbm, wg_hbm,
    xp, gp, og, w, feats, fwd, adj, packs, crecv, res, ing, wg, pair_in, plane_in, plane_sum,
    lon_in, done, share, lines, lsem, ssem, rsem, wssem, wrsem,
):
    members, rows, cols, chan, basis, used, depth, enss, lats, lons, total, scale = dims
    own = rows * cols
    rim = rows * H
    taps = 2 * H + 1
    lat = lax.axis_index("lat")
    lon = lax.axis_index("lon")
    west = lax.rem(lon + lons - 1, lons)
    east = lax.rem(lon + 1, lons)
    has_n = lat > 0
    has_s = lat < lats - 1
    ens = lax.axis_index("ens")
    chips = lats // 2
    plane = enss * chips
    core = lax.rem(lat, 2)
    mine = ens * chips + lat // 2
    held = chan // lons
    chunks, span = wg.shape[0], wg.shape[3]
    piece = span // plane
    group = 2 if members % 2 == 0 else 1
    half = chan // 2

    load_x = pltpu.make_async_copy(x_hbm, xp.at[:, pl.ds(0, own), :], lsem.at[0])
    load_x.start()
    load_og = pltpu.make_async_copy(og_hbm, og, lsem.at[1])
    load_og.start()
    load_w = pltpu.make_async_copy(w_hbm, w, lsem.at[2])
    load_w.start()

    barrier = pltpu.get_barrier_semaphore()

    def greet(where):
        pl.semaphore_signal(barrier, inc=1, device_id=where, device_id_type=MESH)

    greet({"lon": west})
    greet({"lon": east})

    def in_plane(step):
        other = lax.rem(mine + step, plane)
        return {"ens": other // chips, "lat": 2 * lax.rem(other, chips) + core}, other

    def in_group(step):
        other = lax.rem(ens * lats + lat + step, enss * lats)
        return {"ens": other // lats, "lat": lax.rem(other, lats)}

    for hop in range(1, enss * lats):
        greet(in_group(hop))
    for hop in range(1, lons):
        greet({"lon": lax.rem(lon + hop, lons)})

    @pl.when(has_n)
    def _():
        for z in (lon, west, east):
            greet({"lat": lat - 1, "lon": z})

    @pl.when(has_s)
    def _():
        for z in (lon, west, east):
            greet({"lat": lat + 1, "lon": z})

    def clear(pad, land):
        pad[:, used:, :] = jnp.zeros((members, depth - used, chan), BF)

        @pl.when(jnp.logical_not(has_n))
        def _():
            pad[:, own : own + cols, :] = jnp.zeros((members, cols, chan), BF)
            land[0:2] = jnp.zeros((2,) + land.shape[1:], BF)

        @pl.when(jnp.logical_not(has_s))
        def _():
            pad[:, own + cols : own + 2 * cols, :] = jnp.zeros((members, cols, chan), BF)
            land[2:4] = jnp.zeros((2,) + land.shape[1:], BF)

    wide = members * rim
    mh = members * H

    def copies(t):
        pad = (xp, gp)[t]
        pack = packs.at[t]
        land = crecv.at[t]
        top, bottom = pl.ds(own, cols), pl.ds(own + cols, cols)
        left, right = pl.ds(own + 2 * cols, rim), pl.ds(own + 2 * cols + rim, rim)
        corner = lambda q: pack.at[pl.ds(2 * wide + q * mh, mh)]
        north, south = {"lat": lat - 1}, {"lat": lat + 1}
        plan = [
            (pad.at[:, pl.ds(0, cols), :], pad.at[:, bottom, :], north),
            (pad.at[:, pl.ds(own - cols, cols), :], pad.at[:, top, :], south),
            (None, right, {"lon": west}),
            (None, left, {"lon": east}),
            (corner(0), land.at[3], {"lat": lat - 1, "lon": west}),
            (corner(1), land.at[2], {"lat": lat - 1, "lon": east}),
            (corner(2), land.at[1], {"lat": lat + 1, "lon": west}),
            (corner(3), land.at[0], {"lat": lat + 1, "lon": east}),
        ]
        out = {}
        slot = 0
        for q, (src, dst, where) in enumerate(plan):
            if src is None:
                parts = [
                    (pack.at[pl.ds((q - 2) * wide + m * rim, rim)], pad.at[m, dst, :])
                    for m in range(members)
                ]
            else:
                parts = [(src, dst)]
            out[q] = []
            for a, b in parts:
                out[q].append(
                    pltpu.make_async_remote_copy(
                        src_ref=a, dst_ref=b, send_sem=ssem.at[t, slot], recv_sem=rsem.at[t, slot],
                        device_id=where, device_id_type=MESH,
                    )
                )
                slot += 1
        return out

    NORTH, SOUTH, SIDES = (0, 4, 5), (1, 6, 7), (2, 3)

    def each(c, qs, act):
        for q in qs:
            for one in c[q]:
                act(one)

    def send(t):
        c = copies(t)
        pad = (xp, gp)[t]

        ends = []
        for m in range(members):
            got = jnp.dot(
                select_ref[...], pad[m, :own, :], preferred_element_type=F32
            )
            packs[t, m * rim : (m + 1) * rim] = got[:rim].astype(BF)
            packs[t, wide + m * rim : wide + (m + 1) * rim] = got[rim : 2 * rim].astype(BF)
            ends.append(got[2 * rim :])
        packs[t, 2 * wide :] = lax.dot_general(
            regroup_ref[...], jnp.concatenate(ends, 0).astype(BF), (((0,), (0,)), ((), ())),
            preferred_element_type=F32,
        ).astype(BF)
        each(c, SIDES, lambda one: one.start())

        @pl.when(has_n)
        def _():
            each(c, NORTH, lambda one: one.start())

        @pl.when(has_s)
        def _():
            each(c, SOUTH, lambda one: one.start())

    def receive(t):
        c = copies(t)
        pad = (xp, gp)[t]

        each(c, SIDES, lambda one: one.wait_recv())

        @pl.when(has_s)
        def _():
            each(c, NORTH, lambda one: one.wait_recv())

        @pl.when(has_n)
        def _():
            each(c, SOUTH, lambda one: one.wait_recv())

        got = jnp.dot(
            regroup_ref[...], crecv[t].reshape(4 * mh, chan), preferred_element_type=F32
        ).astype(BF)
        for m in range(members):
            pad[m, used - 4 * H : used, :] = got[m * 4 * H : (m + 1) * 4 * H]

    def sent(t):
        c = copies(t)
        each(c, SIDES, lambda one: one.wait_send())

        @pl.when(has_n)
        def _():
            each(c, NORTH, lambda one: one.wait_send())

        @pl.when(has_s)
        def _():
            each(c, SOUTH, lambda one: one.wait_send())

    clear(xp, crecv.at[0])
    clear(gp, crecv.at[1])
    load_x.wait()
    pl.semaphore_wait(
        barrier,
        lons + enss * lats + 3 * has_n.astype(jnp.int32) + 3 * has_s.astype(jnp.int32),
    )
    send(0)

    blocks = basis_ref.shape[2]
    sides = 2 * R + 1
    tall = lines.shape[0] // basis
    eye = (
        lax.broadcasted_iota(jnp.int32, (tall, taps), 0)
        == lax.broadcasted_iota(jnp.int32, (tall, taps), 1)
    ).astype(F32).astype(BF)
    for k in range(basis):
        entries = basis_ref[k].reshape(sides * blocks, taps).astype(BF)
        lines[k * tall : (k + 1) * tall, :] = lax.dot_general(
            eye, entries, (((1,), (1,)), ((), ())), preferred_element_type=F32
        )
    lane = lax.broadcasted_iota(jnp.int32, lines.shape, 1)
    far = jnp.abs(lax.broadcasted_iota(jnp.int32, lines.shape, 0) % tall - H)
    first = lat * rows
    cell_i, cell_j = pos_ref[0:1, :], pos_ref[1:2, :]
    entry = lax.broadcasted_iota(jnp.int32, (sides * blocks, depth), 0)
    offset = entry // blocks
    which = entry % blocks
    col = lax.broadcasted_iota(jnp.int32, (cols, depth), 0)
    ahead = cell_j - col + H
    behind = col - cell_j + H

    def by_side(index, values):
        return jnp.where(index == 0, values[0], jnp.where(index == 1, values[1], values[2]))

    def expand(cycles, wanted, tap, dst, i):
        cycles = [jnp.clip(first + cyc, 0, total - 1) for cyc in cycles]
        span = by_side(lane // blocks, [hw_ref[r, cyc] for r, cyc in enumerate(cycles)])
        table = jnp.where(far <= span, lines[...], 0.0).astype(BF)
        block = by_side(offset, [cb_ref[cyc] for cyc in cycles])
        hit = jnp.logical_and(wanted == offset, which == block)
        spread = jnp.dot(
            table, jnp.where(hit, 1.0, 0.0).astype(BF), preferred_element_type=F32
        )
        for k in range(basis):
            acc = jnp.zeros((cols, depth), F32)
            for d in range(taps):
                line = spread[k * tall + d : k * tall + d + 1, :]
                acc = jnp.where(tap == d, line, acc)
            dst[pl.ds(pl.multiple_of(k * own + i * cols, cols), cols), :] = acc.astype(BF)

    def build_forward(i, carry):
        expand([i] * sides, cell_i - i + R, ahead, fwd, i)
        return carry

    def build_adjoint(i, carry):
        expand([i + R - r for r in range(sides)], i + R - cell_i, behind, adj, i)
        return carry

    lax.fori_loop(0, rows, build_forward, 0)

    def spread_some(mat, pad, begin, end):
        def one(m, carry):
            block = pad[m]
            at = pl.ds(pl.multiple_of(m * own, own), own)
            for k in range(basis):
                feats[at, k * chan : (k + 1) * chan] = jnp.dot(
                    mat[k * own : (k + 1) * own, :], block, preferred_element_type=F32
                ).astype(BF)
            return carry

        lax.fori_loop(begin, end, one, 0)

    receive(0)
    spread_some(fwd, xp, 0, members)
    load_w.wait()
    load_og.wait()

    def forward(n, carry):
        at = pl.ds(pl.multiple_of(n * (group * own), own), group * own)
        v = jnp.dot(
            feats[at, :], w[...].reshape(basis * chan, chan), preferred_element_type=F32
        )
        root = math.sqrt(2.0 / math.pi)
        vv = v * v
        th = jnp.tanh(root * (v + 0.044715 * (vv * v)))
        half_up = 0.5 * (1.0 + th)
        act = v * half_up
        slope = half_up + 0.5 * v * (1.0 - th * th) * (root * (1.0 + 3 * 0.044715 * vv))
        for g in range(group):
            m = n * group + g
            rows_g = slice(g * own, (g + 1) * own)
            res[m] = (xp[m, :own, :].astype(F32) + act[rows_g]).astype(BF)
            gp[m, :own, :] = (og[m].astype(F32) * slope[rows_g]).astype(BF)
        return carry

    lax.fori_loop(0, members // group, forward, 0)
    send(1)
    save_res = pltpu.make_async_copy(res, res_hbm, lsem.at[3])
    save_res.start()

    grad = gp[:, :own, :].reshape(members * own, chan)
    some = basis // chunks

    def mix(n):
        for u in range(some):
            k = n * some + u
            part = lax.dot_general(
                feats[:, k * chan : (k + 1) * chan], grad, (((0,), (0,)), ((), ())),
                preferred_element_type=F32,
            )
            part = (part * scale).astype(wg.dtype)
            for z in range(lons):
                for h in range(2):
                    wg[n, h, z, u * held : (u + 1) * held, :] = part[
                        z * held : (z + 1) * held, h * half : (h + 1) * half
                    ]

    def push(n, src, dst, slot, where):
        one = pltpu.make_async_remote_copy(
            src_ref=src, dst_ref=dst, send_sem=wssem.at[n, slot], recv_sem=wrsem.at[n, slot],
            device_id=where, device_id_type=MESH,
        )
        one.start()
        return one

    own_piece = pl.ds(pl.multiple_of(mine * piece, 16), piece)
    flight = {}

    def to_pair(n):
        flight[n, 0] = [
            push(n, wg.at[n, 1 - core], pair_in.at[n], 0, {"lat": lat + 1 - 2 * core})
        ]

    def arrived(n, stage):
        for one in flight[n, stage]:
            one.wait_recv()

    def to_plane(n):
        arrived(n, 0)

        def add(z, carry):
            wg[n, core, z] = (wg[n, core, z].astype(F32) + pair_in[n, z].astype(F32)).astype(BF)
            return carry

        lax.fori_loop(0, lons, add, 0)
        flight[n, 1] = []
        for hop in range(1, plane):
            where, other = in_plane(hop)
            at = pl.ds(pl.multiple_of(other * piece, 16), piece)
            flight[n, 1].append(
                push(n, wg.at[n, core, :, at, :], plane_in.at[n, hop - 1], hop, where)
            )

    def to_lon(n):
        arrived(n, 1)

        def add(z, carry):
            acc = wg[n, core, z, own_piece, :].astype(F32)
            for hop in range(plane - 1):
                acc = acc + plane_in[n, hop, z].astype(F32)
            plane_sum[n, z] = acc.astype(BF)
            return carry

        lax.fori_loop(0, lons, add, 0)
        flight[n, 2] = []
        for hop in range(1, lons):
            other = lax.rem(lon + hop, lons)
            flight[n, 2].append(
                push(
                    n, plane_sum.at[n, other], lon_in.at[n, hop - 1], plane - 1 + hop,
                    {"lon": other},
                )
            )

    def to_group(n):
        arrived(n, 2)
        acc = plane_sum[n, lon].astype(F32)
        for hop in range(lons - 1):
            acc = acc + lon_in[n, hop].astype(F32)
        done[n, core, own_piece, :] = acc.astype(BF)
        spot = done.at[n, core, own_piece, :]
        flight[n, 3] = [
            push(n, spot, spot, plane + lons - 2 + hop, in_group(hop))
            for hop in range(1, enss * lats)
        ]

    def keep(n):
        arrived(n, 3)
        for h in range(2):
            full = done[n, h].astype(F32)
            for u in range(some):
                share[n * some + u, :, h * half : (h + 1) * half] = full[
                    u * held : (u + 1) * held
                ]

    def backward(n, carry):
        at = pl.ds(pl.multiple_of(n * (group * own), own), group * own)
        acc = None
        for k in range(basis):
            term = lax.dot_general(
                feats[at, k * chan : (k + 1) * chan], w[k], (((1,), (1,)), ((), ())),
                preferred_element_type=F32,
            )
            acc = term if acc is None else acc + term
        for g in range(group):
            m = n * group + g
            ing[m] = (og[m].astype(F32) + acc[g * own : (g + 1) * own]).astype(BF)
        return carry

    for n in range(chunks):
        mix(n)
        to_pair(n)
        if n:
            to_plane(n - 1)
    lax.fori_loop(0, rows, build_adjoint, 0)
    to_plane(chunks - 1)
    receive(1)
    spread_some(adj, gp, 0, members // 2)
    to_lon(0)
    spread_some(adj, gp, members // 2, members)
    for n in range(1, chunks - 1):
        to_lon(n)
    lax.fori_loop(0, members // group, backward, 0)
    save_ing = pltpu.make_async_copy(ing, ing_hbm, lsem.at[5])
    save_ing.start()
    to_group(0)
    if chunks > 1:
        to_lon(chunks - 1)
    for n in range(1, chunks):
        to_group(n)
    sent(0)
    sent(1)
    save_res.wait()
    for n in range(chunks):
        keep(n)
    save_wg = pltpu.make_async_copy(share, wg_hbm, lsem.at[4])
    save_wg.start()
    for copies_sent in flight.values():
        for one in copies_sent:
            one.wait_send()
    save_ing.wait()
    save_wg.wait()


def shards(members_in, out_grad, weight, basis_blocks, cycle_block, half_width):
    members, rows, cols, chan = members_in.shape
    blocks, basis, reach, taps = basis_blocks.shape
    own = rows * cols
    enss, lats, lons = (lax.axis_size(axis) for axis in ("ens", "lat", "lon"))
    plane = enss * lats // 2
    held = chan // lons
    chunks = 3 if basis % 3 == 0 else 1
    span = -(-(basis // chunks) * held // (16 * plane)) * 16 * plane
    piece = span // plane
    half = chan // 2
    used, depth, pos, select, regroup = layout(members, rows, cols)
    tall = -(-taps // 16) * 16
    cell_count = members * enss * own * lats * lons
    dims = (
        members, rows, cols, chan, basis, used, depth, enss, lats, lons, cycle_block.shape[0],
        1.0 / math.sqrt(cell_count),
    )
    anywhere = pl.BlockSpec(memory_space=pl.ANY)
    hbm = pl.BlockSpec(memory_space=pltpu.HBM)
    vmem = pl.BlockSpec(memory_space=pltpu.VMEM)
    smem = pl.BlockSpec(memory_space=pltpu.SMEM)
    cells = (members, own, chan)
    padded = (members, depth, chan)
    slots = 6 + 2 * members
    pushes = plane + lons - 1 + enss * lats - 1
    res, ing, weight_grad = pl.pallas_call(
        functools.partial(block_kernel, dims),
        out_shape=[
            jax.ShapeDtypeStruct(cells, BF),
            jax.ShapeDtypeStruct(cells, BF),
            jax.ShapeDtypeStruct((basis, held, chan), F32),
        ],
        in_specs=[hbm] * 3 + [vmem, smem, smem] + [vmem] * 3,
        out_specs=[anywhere] * 3,
        scratch_shapes=[
            pltpu.VMEM(padded, BF),
            pltpu.VMEM(padded, BF),
            pltpu.VMEM(cells, BF),
            pltpu.VMEM((basis, chan, chan), BF),
            pltpu.VMEM((members * own, basis * chan), BF),
            pltpu.VMEM((basis * own, depth), BF),
            pltpu.VMEM((basis * own, depth), BF),
            pltpu.VMEM((2, members * select.shape[0], chan), BF),
            pltpu.VMEM((2, 4, members * H, chan), BF),
            pltpu.VMEM(cells, BF),
            pltpu.VMEM(cells, BF),
            pltpu.VMEM((chunks, 2, lons, span, half), BF),
            pltpu.VMEM((chunks, lons, span, half), BF),
            pltpu.VMEM((chunks, plane - 1, lons, piece, half), BF),
            pltpu.VMEM((chunks, lons, piece, half), BF),
            pltpu.VMEM((chunks, lons - 1, piece, half), BF),
            pltpu.VMEM((chunks, 2, span, half), BF),
            pltpu.VMEM((basis, held, chan), F32),
            pltpu.VMEM((basis * tall, reach * blocks), F32),
            pltpu.SemaphoreType.DMA((6,)),
            pltpu.SemaphoreType.DMA((2, slots)),
            pltpu.SemaphoreType.DMA((2, slots)),
            pltpu.SemaphoreType.DMA((chunks, pushes)),
            pltpu.SemaphoreType.DMA((chunks, pushes)),
        ],
        compiler_params=pltpu.CompilerParams(
            collective_id=0, has_side_effects=True, vmem_limit_bytes=48 * 1024 * 1024
        ),
    )(
        members_in.reshape(cells), out_grad.reshape(cells), weight,
        jnp.transpose(basis_blocks, (1, 2, 0, 3)), cycle_block, half_width.T,
        jnp.asarray(pos), jnp.asarray(select, dtype=BF), jnp.asarray(regroup, dtype=BF),
    )
    return (res.reshape(members_in.shape), ing.reshape(members_in.shape), weight_grad)


def solution(mesh):
    cells = P("ens", "lat", "lon", None)
    return jax.shard_map(
        shards,
        mesh=mesh,
        in_specs=(cells, cells, P(), P(), P(), P()),
        out_specs=(cells, cells, P(None, "lon", None)),
        check_vma=False,
    )
```

```python
import functools
import math

import jax
import jax.numpy as jnp
import numpy as np
from jax import lax
from jax.experimental import pallas as pl
from jax.experimental.pallas import tpu as pltpu
from jax.sharding import PartitionSpec as P

R = 1
H = 4
VMEM = 63 * 1024 * 1024
MESH = pl.DeviceIdType.MESH
BF = jnp.bfloat16
F32 = jnp.float32


def layout(members, rows, cols):
    cells = [(i, j) for i in range(rows) for j in range(cols)]
    cells += [(-1, j) for j in range(cols)] + [(rows, j) for j in range(cols)]
    cells += [(i, j - H) for i in range(rows) for j in range(H)]
    cells += [(i, cols + j) for i in range(rows) for j in range(H)]
    for i in (-1, rows):
        for first in (-H, cols):
            cells += [(i, first + j) for j in range(H)]
    depth = -(-len(cells) // 128) * 128
    pos = np.full((8, depth), -1000, np.int32)
    for p, (i, j) in enumerate(cells):
        pos[0, p], pos[1, p] = i, j
    own = rows * cols
    picks = [i * cols + j for i in range(rows) for j in range(H)]
    picks += [i * cols + cols - H + j for i in range(rows) for j in range(H)]
    picks += [i * cols + f + j for i in (0, rows - 1) for f in (0, cols - H) for j in range(H)]
    select = np.zeros((len(picks), own), np.float32)
    select[np.arange(len(picks)), picks] = 1
    corners = 4 * members * H
    regroup = np.zeros((corners, corners), np.float32)
    for m in range(members):
        for q in range(4):
            for j in range(H):
                regroup[(m * 4 + q) * H + j, (q * members + m) * H + j] = 1
    return len(cells), depth, pos, select, regroup


def block_kernel(
    dims,
    x_hbm, og_hbm, w_hbm, basis_hbm, cb_ref, hw_ref, pos_hbm, select_hbm, regroup_hbm,
    res_hbm, ing_hbm, wg_hbm,
    xp, gp, og, w, feats, fwd, adj, packs, crecv, res, ing, wg, pair_in, plane_in, plane_sum,
    lon_in, done, share, lines,
    basis_ref, pos_ref, select_ref, regroup_ref, lsem, ssem, rsem, wssem, wrsem,
):
    members, rows, cols, chan, basis, used, depth, enss, lats, lons, total, scale = dims
    own = rows * cols
    rim = rows * H
    taps = 2 * H + 1
    lat = lax.axis_index("lat")
    lon = lax.axis_index("lon")
    west = lax.rem(lon + lons - 1, lons)
    east = lax.rem(lon + 1, lons)
    has_n = lat > 0
    has_s = lat < lats - 1
    ens = lax.axis_index("ens")
    chips = lats // 2
    plane = enss * chips
    core = lax.rem(lat, 2)
    mine = ens * chips + lat // 2
    held = chan // lons
    chunks, span = wg.shape[0], wg.shape[3]
    piece = span // plane
    group = 2 if members % 2 == 0 else 1
    half = chan // 2

    load_x = pltpu.make_async_copy(x_hbm, xp.at[:, pl.ds(0, own), :], lsem.at[0])
    load_x.start()
    loads = [
        pltpu.make_async_copy(src, dst, lsem.at[6 + n])
        for n, (src, dst) in enumerate(
            [
                (select_hbm, select_ref), (regroup_hbm, regroup_ref),
                (basis_hbm, basis_ref), (pos_hbm, pos_ref),
            ]
        )
    ]
    for one in loads:
        one.start()
    load_og = pltpu.make_async_copy(og_hbm, og, lsem.at[1])
    load_og.start()
    load_w = pltpu.make_async_copy(w_hbm, w, lsem.at[2])
    load_w.start()

    barrier = pltpu.get_barrier_semaphore()

    def greet(where):
        pl.semaphore_signal(barrier, inc=1, device_id=where, device_id_type=MESH)

    greet({"lon": west})
    greet({"lon": east})

    def in_plane(step):
        other = lax.rem(mine + step, plane)
        return {"ens": other // chips, "lat": 2 * lax.rem(other, chips) + core}, other

    def in_group(step):
        other = lax.rem(ens * lats + lat + step, enss * lats)
        return {"ens": other // lats, "lat": lax.rem(other, lats)}

    for hop in range(1, enss * lats):
        greet(in_group(hop))
    for hop in range(1, lons):
        greet({"lon": lax.rem(lon + hop, lons)})

    @pl.when(has_n)
    def _():
        for z in (lon, west, east):
            greet({"lat": lat - 1, "lon": z})

    @pl.when(has_s)
    def _():
        for z in (lon, west, east):
            greet({"lat": lat + 1, "lon": z})

    def clear(pad, land):
        pad[:, used:, :] = jnp.zeros((members, depth - used, chan), BF)

        @pl.when(jnp.logical_not(has_n))
        def _():
            pad[:, own : own + cols, :] = jnp.zeros((members, cols, chan), BF)
            land[0:2] = jnp.zeros((2,) + land.shape[1:], BF)

        @pl.when(jnp.logical_not(has_s))
        def _():
            pad[:, own + cols : own + 2 * cols, :] = jnp.zeros((members, cols, chan), BF)
            land[2:4] = jnp.zeros((2,) + land.shape[1:], BF)

    wide = members * rim
    mh = members * H

    def copies(t):
        pad = (xp, gp)[t]
        pack = packs.at[t]
        land = crecv.at[t]
        top, bottom = pl.ds(own, cols), pl.ds(own + cols, cols)
        left, right = pl.ds(own + 2 * cols, rim), pl.ds(own + 2 * cols + rim, rim)
        corner = lambda q: pack.at[pl.ds(2 * wide + q * mh, mh)]
        north, south = {"lat": lat - 1}, {"lat": lat + 1}
        plan = [
            (pad.at[:, pl.ds(0, cols), :], pad.at[:, bottom, :], north),
            (pad.at[:, pl.ds(own - cols, cols), :], pad.at[:, top, :], south),
            (None, right, {"lon": west}),
            (None, left, {"lon": east}),
            (corner(0), land.at[3], {"lat": lat - 1, "lon": west}),
            (corner(1), land.at[2], {"lat": lat - 1, "lon": east}),
            (corner(2), land.at[1], {"lat": lat + 1, "lon": west}),
            (corner(3), land.at[0], {"lat": lat + 1, "lon": east}),
        ]
        out = {}
        slot = 0
        for q, (src, dst, where) in enumerate(plan):
            if src is None:
                parts = [
                    (pack.at[pl.ds((q - 2) * wide + m * rim, rim)], pad.at[m, dst, :])
                    for m in range(members)
                ]
            else:
                parts = [(src, dst)]
            out[q] = []
            for a, b in parts:
                out[q].append(
                    pltpu.make_async_remote_copy(
                        src_ref=a, dst_ref=b, send_sem=ssem.at[t, slot], recv_sem=rsem.at[t, slot],
                        device_id=where, device_id_type=MESH,
                    )
                )
                slot += 1
        return out

    NORTH, SOUTH, SIDES = (0, 4, 5), (1, 6, 7), (2, 3)

    def each(c, qs, act):
        for q in qs:
            for one in c[q]:
                act(one)

    def send(t):
        c = copies(t)
        pad = (xp, gp)[t]

        ends = []
        for m in range(members):
            got = jnp.dot(
                select_ref[...], pad[m, :own, :], preferred_element_type=F32
            )
            packs[t, m * rim : (m + 1) * rim] = got[:rim].astype(BF)
            packs[t, wide + m * rim : wide + (m + 1) * rim] = got[rim : 2 * rim].astype(BF)
            ends.append(got[2 * rim :])
        packs[t, 2 * wide :] = lax.dot_general(
            regroup_ref[...], jnp.concatenate(ends, 0).astype(BF), (((0,), (0,)), ((), ())),
            preferred_element_type=F32,
        ).astype(BF)
        each(c, SIDES, lambda one: one.start())

        @pl.when(has_n)
        def _():
            each(c, NORTH, lambda one: one.start())

        @pl.when(has_s)
        def _():
            each(c, SOUTH, lambda one: one.start())

    def receive(t):
        c = copies(t)
        pad = (xp, gp)[t]

        each(c, SIDES, lambda one: one.wait_recv())

        @pl.when(has_s)
        def _():
            each(c, NORTH, lambda one: one.wait_recv())

        @pl.when(has_n)
        def _():
            each(c, SOUTH, lambda one: one.wait_recv())

        got = jnp.dot(
            regroup_ref[...], crecv[t].reshape(4 * mh, chan), preferred_element_type=F32
        ).astype(BF)
        for m in range(members):
            pad[m, used - 4 * H : used, :] = got[m * 4 * H : (m + 1) * 4 * H]

    def sent(t):
        c = copies(t)
        each(c, SIDES, lambda one: one.wait_send())

        @pl.when(has_n)
        def _():
            each(c, NORTH, lambda one: one.wait_send())

        @pl.when(has_s)
        def _():
            each(c, SOUTH, lambda one: one.wait_send())

    clear(xp, crecv.at[0])
    clear(gp, crecv.at[1])
    load_x.wait()
    for one in loads:
        one.wait()
    pl.semaphore_wait(
        barrier,
        lons + enss * lats + 3 * has_n.astype(jnp.int32) + 3 * has_s.astype(jnp.int32),
    )
    send(0)

    blocks = basis_ref.shape[2]
    sides = 2 * R + 1
    tall = lines.shape[0] // basis
    eye = (
        lax.broadcasted_iota(jnp.int32, (tall, taps), 0)
        == lax.broadcasted_iota(jnp.int32, (tall, taps), 1)
    ).astype(F32).astype(BF)
    for k in range(basis):
        entries = basis_ref[k].reshape(sides * blocks, taps).astype(BF)
        lines[k * tall : (k + 1) * tall, :] = lax.dot_general(
            eye, entries, (((1,), (1,)), ((), ())), preferred_element_type=F32
        )
    lane = lax.broadcasted_iota(jnp.int32, lines.shape, 1)
    far = jnp.abs(lax.broadcasted_iota(jnp.int32, lines.shape, 0) % tall - H)
    first = lat * rows
    cell_i, cell_j = pos_ref[0:1, :], pos_ref[1:2, :]
    entry = lax.broadcasted_iota(jnp.int32, (sides * blocks, depth), 0)
    offset = entry // blocks
    which = entry % blocks
    col = lax.broadcasted_iota(jnp.int32, (cols, depth), 0)
    ahead = cell_j - col + H
    behind = col - cell_j + H

    def by_side(index, values):
        return jnp.where(index == 0, values[0], jnp.where(index == 1, values[1], values[2]))

    def expand(cycles, wanted, tap, dst, i):
        cycles = [jnp.clip(first + cyc, 0, total - 1) for cyc in cycles]
        span = by_side(lane // blocks, [hw_ref[r, cyc] for r, cyc in enumerate(cycles)])
        table = jnp.where(far <= span, lines[...], 0.0).astype(BF)
        block = by_side(offset, [cb_ref[cyc] for cyc in cycles])
        hit = jnp.logical_and(wanted == offset, which == block)
        spread = jnp.dot(
            table, jnp.where(hit, 1.0, 0.0).astype(BF), preferred_element_type=F32
        )
        for k in range(basis):
            acc = jnp.zeros((cols, depth), F32)
            for d in range(taps):
                line = spread[k * tall + d : k * tall + d + 1, :]
                acc = jnp.where(tap == d, line, acc)
            dst[pl.ds(pl.multiple_of(k * own + i * cols, cols), cols), :] = acc.astype(BF)

    def build_forward(i, carry):
        expand([i] * sides, cell_i - i + R, ahead, fwd, i)
        return carry

    def build_adjoint(i, carry):
        expand([i + R - r for r in range(sides)], i + R - cell_i, behind, adj, i)
        return carry

    lax.fori_loop(0, rows, build_forward, 0)

    def spread_some(mat, pad, begin, end):
        def one(m, carry):
            block = pad[m]
            at = pl.ds(pl.multiple_of(m * own, own), own)
            for k in range(basis):
                feats[at, k * chan : (k + 1) * chan] = jnp.dot(
                    mat[k * own : (k + 1) * own, :], block, preferred_element_type=F32
                ).astype(BF)
            return carry

        lax.fori_loop(begin, end, one, 0)

    receive(0)
    spread_some(fwd, xp, 0, members)
    load_w.wait()
    load_og.wait()

    def forward(n, carry):
        at = pl.ds(pl.multiple_of(n * (group * own), own), group * own)
        v = jnp.dot(
            feats[at, :], w[...].reshape(basis * chan, chan), preferred_element_type=F32
        )
        root = math.sqrt(2.0 / math.pi)
        vv = v * v
        th = jnp.tanh(root * (v + 0.044715 * (vv * v)))
        half_up = 0.5 * (1.0 + th)
        act = v * half_up
        slope = half_up + 0.5 * v * (1.0 - th * th) * (root * (1.0 + 3 * 0.044715 * vv))
        for g in range(group):
            m = n * group + g
            rows_g = slice(g * own, (g + 1) * own)
            res[m] = (xp[m, :own, :].astype(F32) + act[rows_g]).astype(BF)
            gp[m, :own, :] = (og[m].astype(F32) * slope[rows_g]).astype(BF)
        return carry

    lax.fori_loop(0, members // group, forward, 0)
    send(1)
    save_res = pltpu.make_async_copy(res, res_hbm, lsem.at[3])
    save_res.start()

    grad = gp[:, :own, :].reshape(members * own, chan)
    some = basis // chunks

    def mix(n):
        for u in range(some):
            k = n * some + u
            part = lax.dot_general(
                feats[:, k * chan : (k + 1) * chan], grad, (((0,), (0,)), ((), ())),
                preferred_element_type=F32,
            )
            part = (part * scale).astype(wg.dtype)
            for z in range(lons):
                for h in range(2):
                    wg[n, h, z, u * held : (u + 1) * held, :] = part[
                        z * held : (z + 1) * held, h * half : (h + 1) * half
                    ]

    def push(n, src, dst, slot, where):
        one = pltpu.make_async_remote_copy(
            src_ref=src, dst_ref=dst, send_sem=wssem.at[n, slot], recv_sem=wrsem.at[n, slot],
            device_id=where, device_id_type=MESH,
        )
        one.start()
        return one

    own_piece = pl.ds(pl.multiple_of(mine * piece, 16), piece)
    flight = {}

    def to_pair(n):
        flight[n, 0] = [
            push(n, wg.at[n, 1 - core], pair_in.at[n], 0, {"lat": lat + 1 - 2 * core})
        ]

    def arrived(n, stage):
        for one in flight[n, stage]:
            one.wait_recv()

    def to_plane(n):
        arrived(n, 0)

        def add(z, carry):
            wg[n, core, z] = (wg[n, core, z].astype(F32) + pair_in[n, z].astype(F32)).astype(BF)
            return carry

        lax.fori_loop(0, lons, add, 0)
        flight[n, 1] = []
        for hop in range(1, plane):
            where, other = in_plane(hop)
            at = pl.ds(pl.multiple_of(other * piece, 16), piece)
            flight[n, 1].append(
                push(n, wg.at[n, core, :, at, :], plane_in.at[n, hop - 1], hop, where)
            )

    def to_lon(n):
        arrived(n, 1)

        def add(z, carry):
            acc = wg[n, core, z, own_piece, :].astype(F32)
            for hop in range(plane - 1):
                acc = acc + plane_in[n, hop, z].astype(F32)
            plane_sum[n, z] = acc.astype(BF)
            return carry

        lax.fori_loop(0, lons, add, 0)
        flight[n, 2] = []
        for hop in range(1, lons):
            other = lax.rem(lon + hop, lons)
            flight[n, 2].append(
                push(
                    n, plane_sum.at[n, other], lon_in.at[n, hop - 1], plane - 1 + hop,
                    {"lon": other},
                )
            )

    def to_group(n):
        arrived(n, 2)
        acc = plane_sum[n, lon].astype(F32)
        for hop in range(lons - 1):
            acc = acc + lon_in[n, hop].astype(F32)
        done[n, core, own_piece, :] = acc.astype(BF)
        spot = done.at[n, core, own_piece, :]
        flight[n, 3] = [
            push(n, spot, spot, plane + lons - 2 + hop, in_group(hop))
            for hop in range(1, enss * lats)
        ]

    def keep(n):
        arrived(n, 3)
        for h in range(2):
            full = done[n, h].astype(F32)
            for u in range(some):
                share[n * some + u, :, h * half : (h + 1) * half] = full[
                    u * held : (u + 1) * held
                ]

    def backward(n, carry):
        at = pl.ds(pl.multiple_of(n * (group * own), own), group * own)
        acc = None
        for k in range(basis):
            term = lax.dot_general(
                feats[at, k * chan : (k + 1) * chan], w[k], (((1,), (1,)), ((), ())),
                preferred_element_type=F32,
            )
            acc = term if acc is None else acc + term
        for g in range(group):
            m = n * group + g
            ing[m] = (og[m].astype(F32) + acc[g * own : (g + 1) * own]).astype(BF)
        return carry

    for n in range(chunks):
        mix(n)
        to_pair(n)
        if n:
            to_plane(n - 1)
    lax.fori_loop(0, rows, build_adjoint, 0)
    to_plane(chunks - 1)
    receive(1)
    spread_some(adj, gp, 0, members // 2)
    to_lon(0)
    spread_some(adj, gp, members // 2, members)
    for n in range(1, chunks - 1):
        to_lon(n)
    lax.fori_loop(0, members // group, backward, 0)
    save_ing = pltpu.make_async_copy(ing, ing_hbm, lsem.at[5])
    save_ing.start()
    to_group(0)
    if chunks > 1:
        to_lon(chunks - 1)
    for n in range(1, chunks):
        to_group(n)
    sent(0)
    sent(1)
    save_res.wait()
    for n in range(chunks):
        keep(n)
    save_wg = pltpu.make_async_copy(share, wg_hbm, lsem.at[4])
    save_wg.start()
    for copies_sent in flight.values():
        for one in copies_sent:
            one.wait_send()
    save_ing.wait()
    save_wg.wait()


def shards(members_in, out_grad, weight, basis_blocks, cycle_block, half_width):
    members, rows, cols, chan = members_in.shape
    blocks, basis, reach, taps = basis_blocks.shape
    own = rows * cols
    enss, lats, lons = (lax.axis_size(axis) for axis in ("ens", "lat", "lon"))
    plane = enss * lats // 2
    held = chan // lons
    chunks = 3 if basis % 3 == 0 else 1
    span = -(-(basis // chunks) * held // (16 * plane)) * 16 * plane
    piece = span // plane
    half = chan // 2
    used, depth, pos, select, regroup = layout(members, rows, cols)
    tall = -(-taps // 16) * 16
    cell_count = members * enss * own * lats * lons
    dims = (
        members, rows, cols, chan, basis, used, depth, enss, lats, lons, cycle_block.shape[0],
        1.0 / math.sqrt(cell_count),
    )
    anywhere = pl.BlockSpec(memory_space=pl.ANY)
    hbm = pl.BlockSpec(memory_space=pltpu.HBM)
    smem = pl.BlockSpec(memory_space=pltpu.SMEM)
    cells = (members, own, chan)
    padded = (members, depth, chan)
    slots = 6 + 2 * members
    pushes = plane + lons - 1 + enss * lats - 1
    res, ing, weight_grad = pl.pallas_call(
        functools.partial(block_kernel, dims),
        out_shape=[
            jax.ShapeDtypeStruct(cells, BF),
            jax.ShapeDtypeStruct(cells, BF),
            jax.ShapeDtypeStruct((basis, held, chan), F32),
        ],
        in_specs=[hbm] * 4 + [smem, smem] + [hbm] * 3,
        out_specs=[anywhere] * 3,
        scratch_shapes=[
            pltpu.VMEM(padded, BF),
            pltpu.VMEM(padded, BF),
            pltpu.VMEM(cells, BF),
            pltpu.VMEM((basis, chan, chan), BF),
            pltpu.VMEM((members * own, basis * chan), BF),
            pltpu.VMEM((basis * own, depth), BF),
            pltpu.VMEM((basis * own, depth), BF),
            pltpu.VMEM((2, members * select.shape[0], chan), BF),
            pltpu.VMEM((2, 4, members * H, chan), BF),
            pltpu.VMEM(cells, BF),
            pltpu.VMEM(cells, BF),
            pltpu.VMEM((chunks, 2, lons, span, half), BF),
            pltpu.VMEM((chunks, lons, span, half), BF),
            pltpu.VMEM((chunks, plane - 1, lons, piece, half), BF),
            pltpu.VMEM((chunks, lons, piece, half), BF),
            pltpu.VMEM((chunks, lons - 1, piece, half), BF),
            pltpu.VMEM((chunks, 2, span, half), BF),
            pltpu.VMEM((basis, held, chan), F32),
            pltpu.VMEM((basis * tall, reach * blocks), F32),
            pltpu.VMEM((basis, reach, blocks, taps), F32),
            pltpu.VMEM(pos.shape, jnp.int32),
            pltpu.VMEM(select.shape, BF),
            pltpu.VMEM(regroup.shape, BF),
            pltpu.SemaphoreType.DMA((10,)),
            pltpu.SemaphoreType.DMA((2, slots)),
            pltpu.SemaphoreType.DMA((2, slots)),
            pltpu.SemaphoreType.DMA((chunks, pushes)),
            pltpu.SemaphoreType.DMA((chunks, pushes)),
        ],
        compiler_params=pltpu.CompilerParams(
            collective_id=0, has_side_effects=True, vmem_limit_bytes=VMEM
        ),
    )(
        members_in.reshape(cells), out_grad.reshape(cells), weight,
        jnp.transpose(basis_blocks, (1, 2, 0, 3)), cycle_block, half_width.T,
        jnp.asarray(pos), jnp.asarray(select, dtype=BF), jnp.asarray(regroup, dtype=BF),
    )
    return (res.reshape(members_in.shape), ing.reshape(members_in.shape), weight_grad)


def solution(mesh):
    cells = P("ens", "lat", "lon", None)
    return jax.shard_map(
        shards,
        mesh=mesh,
        in_specs=(cells, cells, P(), P(), P(), P()),
        out_specs=(cells, cells, P(None, "lon", None)),
        check_vma=False,
    )
```

```python
import functools
import math

import jax
import jax.numpy as jnp
import numpy as np
from jax import lax
from jax.experimental import pallas as pl
from jax.experimental.pallas import tpu as pltpu
from jax.sharding import PartitionSpec as P

R = 1
H = 4
VMEM = 63 * 1024 * 1024
MESH = pl.DeviceIdType.MESH
BF = jnp.bfloat16
F32 = jnp.float32


def layout(members, rows, cols):
    cells = [(i, j) for i in range(rows) for j in range(cols)]
    cells += [(-1, j) for j in range(cols)] + [(rows, j) for j in range(cols)]
    cells += [(i, j - H) for i in range(rows) for j in range(H)]
    cells += [(i, cols + j) for i in range(rows) for j in range(H)]
    for i in (-1, rows):
        for first in (-H, cols):
            cells += [(i, first + j) for j in range(H)]
    depth = -(-len(cells) // 128) * 128
    pos = np.full((8, depth), -1000, np.int32)
    for p, (i, j) in enumerate(cells):
        pos[0, p], pos[1, p] = i, j
    own = rows * cols
    picks = [i * cols + j for i in range(rows) for j in range(H)]
    picks += [i * cols + cols - H + j for i in range(rows) for j in range(H)]
    picks += [i * cols + f + j for i in (0, rows - 1) for f in (0, cols - H) for j in range(H)]
    select = np.zeros((len(picks), own), np.float32)
    select[np.arange(len(picks)), picks] = 1
    corners = 4 * members * H
    regroup = np.zeros((corners, corners), np.float32)
    for m in range(members):
        for q in range(4):
            for j in range(H):
                regroup[(m * 4 + q) * H + j, (q * members + m) * H + j] = 1
    return len(cells), depth, pos, select, regroup


def block_kernel(
    dims,
    x_hbm, og_hbm, w_hbm, basis_hbm, cb_ref, hw_ref, pos_hbm, select_hbm, regroup_hbm,
    res_hbm, ing_hbm, wg_hbm,
    xp, gp, og, w, feats, fwd, adj, packs, crecv, res, ing, wg, pair_in, plane_in, plane_sum,
    lon_in, done, share, lines,
    basis_ref, pos_ref, select_ref, regroup_ref, lsem, ssem, rsem, wssem, wrsem,
):
    members, rows, cols, chan, basis, used, depth, enss, lats, lons, total, scale = dims
    own = rows * cols
    rim = rows * H
    taps = 2 * H + 1
    lat = lax.axis_index("lat")
    lon = lax.axis_index("lon")
    west = lax.rem(lon + lons - 1, lons)
    east = lax.rem(lon + 1, lons)
    has_n = lat > 0
    has_s = lat < lats - 1
    ens = lax.axis_index("ens")
    chips = lats // 2
    plane = enss * chips
    core = lax.rem(lat, 2)
    mine = ens * chips + lat // 2
    held = chan // lons
    chunks, span = wg.shape[0], wg.shape[3]
    piece = span // plane
    group = 2 if members % 2 == 0 else 1
    half = chan // 2

    load_x = pltpu.make_async_copy(x_hbm, xp.at[:, pl.ds(0, own), :], lsem.at[0])
    load_x.start()
    loads = [
        pltpu.make_async_copy(src, dst, lsem.at[6 + n])
        for n, (src, dst) in enumerate(
            [
                (select_hbm, select_ref), (regroup_hbm, regroup_ref),
                (basis_hbm, basis_ref), (pos_hbm, pos_ref),
            ]
        )
    ]
    for one in loads:
        one.start()
    load_og = pltpu.make_async_copy(og_hbm, og, lsem.at[1])
    load_og.start()
    load_w = pltpu.make_async_copy(w_hbm, w, lsem.at[2])
    load_w.start()

    barrier = pltpu.get_barrier_semaphore()

    def greet(where):
        pl.semaphore_signal(barrier, inc=1, device_id=where, device_id_type=MESH)

    greet({"lon": west})
    greet({"lon": east})

    def in_plane(step):
        other = lax.rem(mine + step, plane)
        return {"ens": other // chips, "lat": 2 * lax.rem(other, chips) + core}, other

    def in_group(step):
        other = lax.rem(ens * lats + lat + step, enss * lats)
        return {"ens": other // lats, "lat": lax.rem(other, lats)}

    for hop in range(1, enss * lats):
        greet(in_group(hop))
    for hop in range(1, lons):
        greet({"lon": lax.rem(lon + hop, lons)})

    @pl.when(has_n)
    def _():
        for z in (lon, west, east):
            greet({"lat": lat - 1, "lon": z})

    @pl.when(has_s)
    def _():
        for z in (lon, west, east):
            greet({"lat": lat + 1, "lon": z})

    def clear(pad, land):
        pad[:, used:, :] = jnp.zeros((members, depth - used, chan), BF)

        @pl.when(jnp.logical_not(has_n))
        def _():
            pad[:, own : own + cols, :] = jnp.zeros((members, cols, chan), BF)
            land[0:2] = jnp.zeros((2,) + land.shape[1:], BF)

        @pl.when(jnp.logical_not(has_s))
        def _():
            pad[:, own + cols : own + 2 * cols, :] = jnp.zeros((members, cols, chan), BF)
            land[2:4] = jnp.zeros((2,) + land.shape[1:], BF)

    wide = members * rim
    mh = members * H

    def copies(t):
        pad = (xp, gp)[t]
        pack = packs.at[t]
        land = crecv.at[t]
        top, bottom = pl.ds(own, cols), pl.ds(own + cols, cols)
        left, right = pl.ds(own + 2 * cols, rim), pl.ds(own + 2 * cols + rim, rim)
        corner = lambda q: pack.at[pl.ds(2 * wide + q * mh, mh)]
        north, south = {"lat": lat - 1}, {"lat": lat + 1}
        plan = [
            (pad.at[:, pl.ds(0, cols), :], pad.at[:, bottom, :], north),
            (pad.at[:, pl.ds(own - cols, cols), :], pad.at[:, top, :], south),
            (None, right, {"lon": west}),
            (None, left, {"lon": east}),
            (corner(0), land.at[3], {"lat": lat - 1, "lon": west}),
            (corner(1), land.at[2], {"lat": lat - 1, "lon": east}),
            (corner(2), land.at[1], {"lat": lat + 1, "lon": west}),
            (corner(3), land.at[0], {"lat": lat + 1, "lon": east}),
        ]
        out = {}
        slot = 0
        for q, (src, dst, where) in enumerate(plan):
            if src is None:
                parts = [
                    (pack.at[pl.ds((q - 2) * wide + m * rim, rim)], pad.at[m, dst, :])
                    for m in range(members)
                ]
            else:
                parts = [(src, dst)]
            out[q] = []
            for a, b in parts:
                out[q].append(
                    pltpu.make_async_remote_copy(
                        src_ref=a, dst_ref=b, send_sem=ssem.at[t, slot], recv_sem=rsem.at[t, slot],
                        device_id=where, device_id_type=MESH,
                    )
                )
                slot += 1
        return out

    NORTH, SOUTH, SIDES = (0, 4, 5), (1, 6, 7), (2, 3)

    def each(c, qs, act):
        for q in qs:
            for one in c[q]:
                act(one)

    def send(t):
        c = copies(t)
        pad = (xp, gp)[t]

        ends = []
        for m in range(members):
            got = jnp.dot(
                select_ref[...], pad[m, :own, :], preferred_element_type=F32
            )
            packs[t, m * rim : (m + 1) * rim] = got[:rim].astype(BF)
            packs[t, wide + m * rim : wide + (m + 1) * rim] = got[rim : 2 * rim].astype(BF)
            ends.append(got[2 * rim :])
        packs[t, 2 * wide :] = lax.dot_general(
            regroup_ref[...], jnp.concatenate(ends, 0).astype(BF), (((0,), (0,)), ((), ())),
            preferred_element_type=F32,
        ).astype(BF)
        each(c, SIDES, lambda one: one.start())

        @pl.when(has_n)
        def _():
            each(c, NORTH, lambda one: one.start())

        @pl.when(has_s)
        def _():
            each(c, SOUTH, lambda one: one.start())

    def receive(t):
        c = copies(t)
        pad = (xp, gp)[t]

        each(c, SIDES, lambda one: one.wait_recv())

        @pl.when(has_s)
        def _():
            each(c, NORTH, lambda one: one.wait_recv())

        @pl.when(has_n)
        def _():
            each(c, SOUTH, lambda one: one.wait_recv())

        got = jnp.dot(
            regroup_ref[...], crecv[t].reshape(4 * mh, chan), preferred_element_type=F32
        ).astype(BF)
        for m in range(members):
            pad[m, used - 4 * H : used, :] = got[m * 4 * H : (m + 1) * 4 * H]

    def sent(t):
        c = copies(t)
        each(c, SIDES, lambda one: one.wait_send())

        @pl.when(has_n)
        def _():
            each(c, NORTH, lambda one: one.wait_send())

        @pl.when(has_s)
        def _():
            each(c, SOUTH, lambda one: one.wait_send())

    clear(xp, crecv.at[0])
    clear(gp, crecv.at[1])
    load_x.wait()
    for one in loads:
        one.wait()
    pl.semaphore_wait(
        barrier,
        lons + enss * lats + 3 * has_n.astype(jnp.int32) + 3 * has_s.astype(jnp.int32),
    )
    send(0)

    blocks = basis_ref.shape[2]
    sides = 2 * R + 1
    tall = lines.shape[0] // basis
    eye = (
        lax.broadcasted_iota(jnp.int32, (tall, taps), 0)
        == lax.broadcasted_iota(jnp.int32, (tall, taps), 1)
    ).astype(F32).astype(BF)
    for k in range(basis):
        entries = basis_ref[k].reshape(sides * blocks, taps).astype(BF)
        lines[k * tall : (k + 1) * tall, :] = lax.dot_general(
            eye, entries, (((1,), (1,)), ((), ())), preferred_element_type=F32
        )
    lane = lax.broadcasted_iota(jnp.int32, lines.shape, 1)
    far = jnp.abs(lax.broadcasted_iota(jnp.int32, lines.shape, 0) % tall - H)
    first = lat * rows
    cell_i, cell_j = pos_ref[0:1, :], pos_ref[1:2, :]
    entry = lax.broadcasted_iota(jnp.int32, (sides * blocks, depth), 0)
    offset = entry // blocks
    which = entry % blocks
    col = lax.broadcasted_iota(jnp.int32, (cols, depth), 0)
    ahead = cell_j - col + H
    behind = col - cell_j + H

    def by_side(index, values):
        return jnp.where(index == 0, values[0], jnp.where(index == 1, values[1], values[2]))

    def expand(cycles, wanted, tap, dst, i):
        cycles = [jnp.clip(first + cyc, 0, total - 1) for cyc in cycles]
        span = by_side(lane // blocks, [hw_ref[r, cyc] for r, cyc in enumerate(cycles)])
        table = jnp.where(far <= span, lines[...], 0.0).astype(BF)
        block = by_side(offset, [cb_ref[cyc] for cyc in cycles])
        hit = jnp.logical_and(wanted == offset, which == block)
        spread = jnp.dot(
            table, jnp.where(hit, 1.0, 0.0).astype(BF), preferred_element_type=F32
        )
        for k in range(basis):
            acc = jnp.zeros((cols, depth), F32)
            for d in range(taps):
                line = spread[k * tall + d : k * tall + d + 1, :]
                acc = jnp.where(tap == d, line, acc)
            dst[pl.ds(pl.multiple_of(k * own + i * cols, cols), cols), :] = acc.astype(BF)

    def build_forward(i, carry):
        expand([i] * sides, cell_i - i + R, ahead, fwd, i)
        return carry

    def build_adjoint(i, carry):
        expand([i + R - r for r in range(sides)], i + R - cell_i, behind, adj, i)
        return carry

    lax.fori_loop(0, rows, build_forward, 0)

    def spread_some(mat, pad, begin, end):
        def one(m, carry):
            block = pad[m]
            at = pl.ds(pl.multiple_of(m * own, own), own)
            for k in range(basis):
                feats[at, k * chan : (k + 1) * chan] = jnp.dot(
                    mat[k * own : (k + 1) * own, :], block, preferred_element_type=F32
                ).astype(BF)
            return carry

        lax.fori_loop(begin, end, one, 0)

    receive(0)
    spread_some(fwd, xp, 0, members)
    load_w.wait()
    load_og.wait()

    def forward(n, carry):
        at = pl.ds(pl.multiple_of(n * (group * own), own), group * own)
        v = jnp.dot(
            feats[at, :], w[...].reshape(basis * chan, chan), preferred_element_type=F32
        )
        root = math.sqrt(2.0 / math.pi)
        vv = v * v
        th = jnp.tanh(root * (v + 0.044715 * (vv * v)))
        half_up = 0.5 * (1.0 + th)
        act = v * half_up
        slope = half_up + 0.5 * v * (1.0 - th * th) * (root * (1.0 + 3 * 0.044715 * vv))
        for g in range(group):
            m = n * group + g
            rows_g = slice(g * own, (g + 1) * own)
            res[m] = (xp[m, :own, :].astype(F32) + act[rows_g]).astype(BF)
            gp[m, :own, :] = (og[m].astype(F32) * slope[rows_g]).astype(BF)
        return carry

    lax.fori_loop(0, members // group, forward, 0)
    send(1)
    save_res = pltpu.make_async_copy(res, res_hbm, lsem.at[3])
    save_res.start()

    grad = gp[:, :own, :].reshape(members * own, chan)
    some = basis // chunks
    unit = (
        lax.broadcasted_iota(jnp.int32, (chan, chan), 0)
        == lax.broadcasted_iota(jnp.int32, (chan, chan), 1)
    ).astype(F32).astype(BF)

    def turn(block):
        return lax.dot_general(
            unit, block, (((1,), (1,)), ((), ())), preferred_element_type=F32
        ).astype(BF)

    turned = turn(grad)

    def mix(n):
        for u in range(some):
            k = n * some + u
            part = jnp.dot(
                turned, feats[:, k * chan : (k + 1) * chan], preferred_element_type=F32
            )
            part = turn((part * scale).astype(BF))
            for z in range(lons):
                for h in range(2):
                    wg[n, h, z, u * held : (u + 1) * held, :] = part[
                        z * held : (z + 1) * held, h * half : (h + 1) * half
                    ]

    def push(n, src, dst, slot, where):
        one = pltpu.make_async_remote_copy(
            src_ref=src, dst_ref=dst, send_sem=wssem.at[n, slot], recv_sem=wrsem.at[n, slot],
            device_id=where, device_id_type=MESH,
        )
        one.start()
        return one

    own_piece = pl.ds(pl.multiple_of(mine * piece, 16), piece)
    flight = {}

    def to_pair(n):
        flight[n, 0] = [
            push(n, wg.at[n, 1 - core], pair_in.at[n], 0, {"lat": lat + 1 - 2 * core})
        ]

    def arrived(n, stage):
        for one in flight[n, stage]:
            one.wait_recv()

    def to_plane(n):
        arrived(n, 0)

        def add(z, carry):
            wg[n, core, z] = (wg[n, core, z].astype(F32) + pair_in[n, z].astype(F32)).astype(BF)
            return carry

        lax.fori_loop(0, lons, add, 0)
        flight[n, 1] = []
        for hop in range(1, plane):
            where, other = in_plane(hop)
            at = pl.ds(pl.multiple_of(other * piece, 16), piece)
            flight[n, 1].append(
                push(n, wg.at[n, core, :, at, :], plane_in.at[n, hop - 1], hop, where)
            )

    def to_lon(n):
        arrived(n, 1)

        def add(z, carry):
            acc = wg[n, core, z, own_piece, :].astype(F32)
            for hop in range(plane - 1):
                acc = acc + plane_in[n, hop, z].astype(F32)
            plane_sum[n, z] = acc.astype(BF)
            return carry

        lax.fori_loop(0, lons, add, 0)
        flight[n, 2] = []
        for hop in range(1, lons):
            other = lax.rem(lon + hop, lons)
            flight[n, 2].append(
                push(
                    n, plane_sum.at[n, other], lon_in.at[n, hop - 1], plane - 1 + hop,
                    {"lon": other},
                )
            )

    def to_group(n):
        arrived(n, 2)
        acc = plane_sum[n, lon].astype(F32)
        for hop in range(lons - 1):
            acc = acc + lon_in[n, hop].astype(F32)
        done[n, core, own_piece, :] = acc.astype(BF)
        spot = done.at[n, core, own_piece, :]
        flight[n, 3] = [
            push(n, spot, spot, plane + lons - 2 + hop, in_group(hop))
            for hop in range(1, enss * lats)
        ]

    def keep(n):
        arrived(n, 3)
        for h in range(2):
            full = done[n, h].astype(F32)
            for u in range(some):
                share[n * some + u, :, h * half : (h + 1) * half] = full[
                    u * held : (u + 1) * held
                ]

    def backward(n, carry):
        at = pl.ds(pl.multiple_of(n * (group * own), own), group * own)
        acc = None
        for k in range(basis):
            term = lax.dot_general(
                feats[at, k * chan : (k + 1) * chan], w[k], (((1,), (1,)), ((), ())),
                preferred_element_type=F32,
            )
            acc = term if acc is None else acc + term
        for g in range(group):
            m = n * group + g
            ing[m] = (og[m].astype(F32) + acc[g * own : (g + 1) * own]).astype(BF)
        return carry

    for n in range(chunks):
        mix(n)
        to_pair(n)
        if n:
            to_plane(n - 1)
    lax.fori_loop(0, rows, build_adjoint, 0)
    to_plane(chunks - 1)
    receive(1)
    spread_some(adj, gp, 0, members // 2)
    to_lon(0)
    spread_some(adj, gp, members // 2, members)
    for n in range(1, chunks - 1):
        to_lon(n)
    turns = members // group
    lax.fori_loop(0, turns // 2, backward, 0)
    to_group(0)
    lax.fori_loop(turns // 2, turns, backward, 0)
    save_ing = pltpu.make_async_copy(ing, ing_hbm, lsem.at[5])
    save_ing.start()
    if chunks > 1:
        to_lon(chunks - 1)
    for n in range(1, chunks):
        to_group(n)
    sent(0)
    sent(1)
    save_res.wait()
    for n in range(chunks):
        keep(n)
    save_wg = pltpu.make_async_copy(share, wg_hbm, lsem.at[4])
    save_wg.start()
    for copies_sent in flight.values():
        for one in copies_sent:
            one.wait_send()
    save_ing.wait()
    save_wg.wait()


def place_kernel(res_in, ing_in, wg_in, res_out, ing_out, wg_out, sem):
    moves = []
    for src, dst in ((res_in, res_out), (ing_in, ing_out), (wg_in, wg_out)):
        for part in range(src.shape[0]):
            moves.append(
                pltpu.make_async_copy(src.at[part], dst.at[part], sem.at[len(moves)])
            )
    for one in moves:
        one.start()
    for one in moves:
        one.wait()


def shards(members_in, out_grad, weight, basis_blocks, cycle_block, half_width):
    members, rows, cols, chan = members_in.shape
    blocks, basis, reach, taps = basis_blocks.shape
    own = rows * cols
    enss, lats, lons = (lax.axis_size(axis) for axis in ("ens", "lat", "lon"))
    plane = enss * lats // 2
    held = chan // lons
    chunks = 3 if basis % 3 == 0 else 1
    span = -(-(basis // chunks) * held // (16 * plane)) * 16 * plane
    piece = span // plane
    half = chan // 2
    used, depth, pos, select, regroup = layout(members, rows, cols)
    tall = -(-taps // 16) * 16
    cell_count = members * enss * own * lats * lons
    dims = (
        members, rows, cols, chan, basis, used, depth, enss, lats, lons, cycle_block.shape[0],
        1.0 / math.sqrt(cell_count),
    )
    anywhere = pl.BlockSpec(memory_space=pl.ANY)
    hbm = pl.BlockSpec(memory_space=pltpu.HBM)
    smem = pl.BlockSpec(memory_space=pltpu.SMEM)
    cells = (members, own, chan)
    padded = (members, depth, chan)
    slots = 6 + 2 * members
    pushes = plane + lons - 1 + enss * lats - 1
    res, ing, weight_grad = pl.pallas_call(
        functools.partial(block_kernel, dims),
        out_shape=[
            jax.ShapeDtypeStruct(cells, BF),
            jax.ShapeDtypeStruct(cells, BF),
            jax.ShapeDtypeStruct((basis, held, chan), F32),
        ],
        in_specs=[hbm] * 4 + [smem, smem] + [hbm] * 3,
        out_specs=[anywhere] * 3,
        scratch_shapes=[
            pltpu.VMEM(padded, BF),
            pltpu.VMEM(padded, BF),
            pltpu.VMEM(cells, BF),
            pltpu.VMEM((basis, chan, chan), BF),
            pltpu.VMEM((members * own, basis * chan), BF),
            pltpu.VMEM((basis * own, depth), BF),
            pltpu.VMEM((basis * own, depth), BF),
            pltpu.VMEM((2, members * select.shape[0], chan), BF),
            pltpu.VMEM((2, 4, members * H, chan), BF),
            pltpu.VMEM(cells, BF),
            pltpu.VMEM(cells, BF),
            pltpu.VMEM((chunks, 2, lons, span, half), BF),
            pltpu.VMEM((chunks, lons, span, half), BF),
            pltpu.VMEM((chunks, plane - 1, lons, piece, half), BF),
            pltpu.VMEM((chunks, lons, piece, half), BF),
            pltpu.VMEM((chunks, lons - 1, piece, half), BF),
            pltpu.VMEM((chunks, 2, span, half), BF),
            pltpu.VMEM((basis, held, chan), F32),
            pltpu.VMEM((basis * tall, reach * blocks), F32),
            pltpu.VMEM((basis, reach, blocks, taps), F32),
            pltpu.VMEM(pos.shape, jnp.int32),
            pltpu.VMEM(select.shape, BF),
            pltpu.VMEM(regroup.shape, BF),
            pltpu.SemaphoreType.DMA((10,)),
            pltpu.SemaphoreType.DMA((2, slots)),
            pltpu.SemaphoreType.DMA((2, slots)),
            pltpu.SemaphoreType.DMA((chunks, pushes)),
            pltpu.SemaphoreType.DMA((chunks, pushes)),
        ],
        compiler_params=pltpu.CompilerParams(
            collective_id=0, has_side_effects=True, vmem_limit_bytes=VMEM
        ),
    )(
        members_in.reshape(cells), out_grad.reshape(cells), weight,
        jnp.transpose(basis_blocks, (1, 2, 0, 3)), cycle_block, half_width.T,
        jnp.asarray(pos), jnp.asarray(select, dtype=BF), jnp.asarray(regroup, dtype=BF),
    )
    held_back = [res, ing, weight_grad]
    res, ing, weight_grad = pl.pallas_call(
        place_kernel,
        out_shape=[jax.ShapeDtypeStruct(a.shape, a.dtype) for a in held_back],
        in_specs=[hbm] * 3,
        out_specs=[hbm] * 3,
        scratch_shapes=[pltpu.SemaphoreType.DMA((sum(a.shape[0] for a in held_back),))],
        compiler_params=pltpu.CompilerParams(vmem_limit_bytes=VMEM),
    )(*held_back)
    return (res.reshape(members_in.shape), ing.reshape(members_in.shape), weight_grad)


def solution(mesh):
    cells = P("ens", "lat", "lon", None)
    return jax.shard_map(
        shards,
        mesh=mesh,
        in_specs=(cells, cells, P(), P(), P(), P()),
        out_specs=(cells, cells, P(None, "lon", None)),
        check_vma=False,
    )
```

```python
import functools
import math

import jax
import jax.numpy as jnp
import numpy as np
from jax import lax
from jax.experimental import pallas as pl
from jax.experimental.pallas import tpu as pltpu
from jax.sharding import PartitionSpec as P

R = 1
H = 4
VMEM = 60 * 1024 * 1024
MESH = pl.DeviceIdType.MESH
BF = jnp.bfloat16
F32 = jnp.float32


def layout(members, rows, cols):
    cells = [(i, j) for i in range(rows) for j in range(cols)]
    cells += [(-1, j) for j in range(cols)] + [(rows, j) for j in range(cols)]
    cells += [(i, j - H) for i in range(rows) for j in range(H)]
    cells += [(i, cols + j) for i in range(rows) for j in range(H)]
    for i in (-1, rows):
        for first in (-H, cols):
            cells += [(i, first + j) for j in range(H)]
    depth = -(-len(cells) // 128) * 128
    pos = np.full((8, depth), -1000, np.int32)
    for p, (i, j) in enumerate(cells):
        pos[0, p], pos[1, p] = i, j
    own = rows * cols
    picks = [i * cols + j for i in range(rows) for j in range(H)]
    picks += [i * cols + cols - H + j for i in range(rows) for j in range(H)]
    picks += [i * cols + f + j for i in (0, rows - 1) for f in (0, cols - H) for j in range(H)]
    select = np.zeros((len(picks), own), np.float32)
    select[np.arange(len(picks)), picks] = 1
    corners = 4 * members * H
    regroup = np.zeros((corners, corners), np.float32)
    for m in range(members):
        for q in range(4):
            for j in range(H):
                regroup[(m * 4 + q) * H + j, (q * members + m) * H + j] = 1
    return len(cells), depth, pos, select, regroup


def block_kernel(
    dims,
    x_hbm, og_hbm, w_hbm, basis_hbm, cb_ref, hw_ref, pos_hbm, select_hbm, regroup_hbm,
    res, ing, share,
    xp, gp, og, w, feats, fwd, adj, packs, crecv, wg, pair_in, plane_in, plane_sum,
    lon_in, done, lines,
    basis_ref, pos_ref, select_ref, regroup_ref, lsem, ssem, rsem, wssem, wrsem,
):
    members, rows, cols, chan, basis, used, depth, enss, lats, lons, total, scale = dims
    own = rows * cols
    rim = rows * H
    taps = 2 * H + 1
    lat = lax.axis_index("lat")
    lon = lax.axis_index("lon")
    west = lax.rem(lon + lons - 1, lons)
    east = lax.rem(lon + 1, lons)
    has_n = lat > 0
    has_s = lat < lats - 1
    ens = lax.axis_index("ens")
    chips = lats // 2
    plane = enss * chips
    core = lax.rem(lat, 2)
    mine = ens * chips + lat // 2
    held = chan // lons
    chunks, span = wg.shape[0], wg.shape[3]
    piece = span // plane
    group = 2 if members % 2 == 0 else 1
    half = chan // 2

    load_x = pltpu.make_async_copy(x_hbm, xp.at[:, pl.ds(0, own), :], lsem.at[0])
    load_x.start()
    loads = [
        pltpu.make_async_copy(src, dst, lsem.at[6 + n])
        for n, (src, dst) in enumerate(
            [
                (select_hbm, select_ref), (regroup_hbm, regroup_ref),
                (basis_hbm, basis_ref), (pos_hbm, pos_ref),
            ]
        )
    ]
    for one in loads:
        one.start()
    load_og = pltpu.make_async_copy(og_hbm, og, lsem.at[1])
    load_og.start()
    load_w = pltpu.make_async_copy(w_hbm, w, lsem.at[2])
    load_w.start()

    barrier = pltpu.get_barrier_semaphore()

    def greet(where):
        pl.semaphore_signal(barrier, inc=1, device_id=where, device_id_type=MESH)

    greet({"lon": west})
    greet({"lon": east})

    def in_plane(step):
        other = lax.rem(mine + step, plane)
        return {"ens": other // chips, "lat": 2 * lax.rem(other, chips) + core}, other

    def in_group(step):
        other = lax.rem(ens * lats + lat + step, enss * lats)
        return {"ens": other // lats, "lat": lax.rem(other, lats)}

    for hop in range(1, enss * lats):
        greet(in_group(hop))
    for hop in range(1, lons):
        greet({"lon": lax.rem(lon + hop, lons)})

    @pl.when(has_n)
    def _():
        for z in (lon, west, east):
            greet({"lat": lat - 1, "lon": z})

    @pl.when(has_s)
    def _():
        for z in (lon, west, east):
            greet({"lat": lat + 1, "lon": z})

    def clear(pad, land):
        pad[:, used:, :] = jnp.zeros((members, depth - used, chan), BF)

        @pl.when(jnp.logical_not(has_n))
        def _():
            pad[:, own : own + cols, :] = jnp.zeros((members, cols, chan), BF)
            land[0:2] = jnp.zeros((2,) + land.shape[1:], BF)

        @pl.when(jnp.logical_not(has_s))
        def _():
            pad[:, own + cols : own + 2 * cols, :] = jnp.zeros((members, cols, chan), BF)
            land[2:4] = jnp.zeros((2,) + land.shape[1:], BF)

    wide = members * rim
    mh = members * H

    def copies(t):
        pad = (xp, gp)[t]
        pack = packs.at[t]
        land = crecv.at[t]
        top, bottom = pl.ds(own, cols), pl.ds(own + cols, cols)
        left, right = pl.ds(own + 2 * cols, rim), pl.ds(own + 2 * cols + rim, rim)
        corner = lambda q: pack.at[pl.ds(2 * wide + q * mh, mh)]
        north, south = {"lat": lat - 1}, {"lat": lat + 1}
        plan = [
            (pad.at[:, pl.ds(0, cols), :], pad.at[:, bottom, :], north),
            (pad.at[:, pl.ds(own - cols, cols), :], pad.at[:, top, :], south),
            (None, right, {"lon": west}),
            (None, left, {"lon": east}),
            (corner(0), land.at[3], {"lat": lat - 1, "lon": west}),
            (corner(1), land.at[2], {"lat": lat - 1, "lon": east}),
            (corner(2), land.at[1], {"lat": lat + 1, "lon": west}),
            (corner(3), land.at[0], {"lat": lat + 1, "lon": east}),
        ]
        out = {}
        slot = 0
        for q, (src, dst, where) in enumerate(plan):
            if src is None:
                parts = [
                    (pack.at[pl.ds((q - 2) * wide + m * rim, rim)], pad.at[m, dst, :])
                    for m in range(members)
                ]
            else:
                parts = [(src, dst)]
            out[q] = []
            for a, b in parts:
                out[q].append(
                    pltpu.make_async_remote_copy(
                        src_ref=a, dst_ref=b, send_sem=ssem.at[t, slot], recv_sem=rsem.at[t, slot],
                        device_id=where, device_id_type=MESH,
                    )
                )
                slot += 1
        return out

    NORTH, SOUTH, SIDES = (0, 4, 5), (1, 6, 7), (2, 3)

    def each(c, qs, act):
        for q in qs:
            for one in c[q]:
                act(one)

    def send(t):
        c = copies(t)
        pad = (xp, gp)[t]

        ends = []
        for m in range(members):
            got = jnp.dot(
                select_ref[...], pad[m, :own, :], preferred_element_type=F32
            )
            packs[t, m * rim : (m + 1) * rim] = got[:rim].astype(BF)
            packs[t, wide + m * rim : wide + (m + 1) * rim] = got[rim : 2 * rim].astype(BF)
            ends.append(got[2 * rim :])
        packs[t, 2 * wide :] = lax.dot_general(
            regroup_ref[...], jnp.concatenate(ends, 0).astype(BF), (((0,), (0,)), ((), ())),
            preferred_element_type=F32,
        ).astype(BF)
        each(c, SIDES, lambda one: one.start())

        @pl.when(has_n)
        def _():
            each(c, NORTH, lambda one: one.start())

        @pl.when(has_s)
        def _():
            each(c, SOUTH, lambda one: one.start())

    def receive(t):
        c = copies(t)
        pad = (xp, gp)[t]

        each(c, SIDES, lambda one: one.wait_recv())

        @pl.when(has_s)
        def _():
            each(c, NORTH, lambda one: one.wait_recv())

        @pl.when(has_n)
        def _():
            each(c, SOUTH, lambda one: one.wait_recv())

        got = jnp.dot(
            regroup_ref[...], crecv[t].reshape(4 * mh, chan), preferred_element_type=F32
        ).astype(BF)
        for m in range(members):
            pad[m, used - 4 * H : used, :] = got[m * 4 * H : (m + 1) * 4 * H]

    def sent(t):
        c = copies(t)
        each(c, SIDES, lambda one: one.wait_send())

        @pl.when(has_n)
        def _():
            each(c, NORTH, lambda one: one.wait_send())

        @pl.when(has_s)
        def _():
            each(c, SOUTH, lambda one: one.wait_send())

    clear(xp, crecv.at[0])
    clear(gp, crecv.at[1])
    load_x.wait()
    for one in loads:
        one.wait()
    pl.semaphore_wait(
        barrier,
        lons + enss * lats + 3 * has_n.astype(jnp.int32) + 3 * has_s.astype(jnp.int32),
    )
    send(0)

    blocks = basis_ref.shape[2]
    sides = 2 * R + 1
    tall = lines.shape[0] // basis
    eye = (
        lax.broadcasted_iota(jnp.int32, (tall, taps), 0)
        == lax.broadcasted_iota(jnp.int32, (tall, taps), 1)
    ).astype(F32).astype(BF)
    for k in range(basis):
        entries = basis_ref[k].reshape(sides * blocks, taps).astype(BF)
        lines[k * tall : (k + 1) * tall, :] = lax.dot_general(
            eye, entries, (((1,), (1,)), ((), ())), preferred_element_type=F32
        )
    lane = lax.broadcasted_iota(jnp.int32, lines.shape, 1)
    far = jnp.abs(lax.broadcasted_iota(jnp.int32, lines.shape, 0) % tall - H)
    first = lat * rows
    cell_i, cell_j = pos_ref[0:1, :], pos_ref[1:2, :]
    entry = lax.broadcasted_iota(jnp.int32, (sides * blocks, depth), 0)
    offset = entry // blocks
    which = entry % blocks
    col = lax.broadcasted_iota(jnp.int32, (cols, depth), 0)
    ahead = cell_j - col + H
    behind = col - cell_j + H

    def by_side(index, values):
        return jnp.where(index == 0, values[0], jnp.where(index == 1, values[1], values[2]))

    def expand(cycles, wanted, tap, dst, i):
        cycles = [jnp.clip(first + cyc, 0, total - 1) for cyc in cycles]
        span = by_side(lane // blocks, [hw_ref[r, cyc] for r, cyc in enumerate(cycles)])
        table = jnp.where(far <= span, lines[...], 0.0).astype(BF)
        block = by_side(offset, [cb_ref[cyc] for cyc in cycles])
        hit = jnp.logical_and(wanted == offset, which == block)
        spread = jnp.dot(
            table, jnp.where(hit, 1.0, 0.0).astype(BF), preferred_element_type=F32
        )
        for k in range(basis):
            acc = jnp.zeros((cols, depth), F32)
            for d in range(taps):
                line = spread[k * tall + d : k * tall + d + 1, :]
                acc = jnp.where(tap == d, line, acc)
            dst[pl.ds(pl.multiple_of(k * own + i * cols, cols), cols), :] = acc.astype(BF)

    def build_forward(i, carry):
        expand([i] * sides, cell_i - i + R, ahead, fwd, i)
        return carry

    def build_adjoint(i, carry):
        expand([i + R - r for r in range(sides)], i + R - cell_i, behind, adj, i)
        return carry

    lax.fori_loop(0, rows, build_forward, 0)

    def spread_some(mat, pad, begin, end):
        def one(m, carry):
            block = pad[m]
            at = pl.ds(pl.multiple_of(m * own, own), own)
            for k in range(basis):
                feats[at, k * chan : (k + 1) * chan] = jnp.dot(
                    mat[k * own : (k + 1) * own, :], block, preferred_element_type=F32
                ).astype(BF)
            return carry

        lax.fori_loop(begin, end, one, 0)

    receive(0)
    spread_some(fwd, xp, 0, members)
    load_w.wait()
    load_og.wait()

    def forward(n, carry):
        at = pl.ds(pl.multiple_of(n * (group * own), own), group * own)
        v = jnp.dot(
            feats[at, :], w[...].reshape(basis * chan, chan), preferred_element_type=F32
        )
        root = math.sqrt(2.0 / math.pi)
        vv = v * v
        th = jnp.tanh(root * (v + 0.044715 * (vv * v)))
        half_up = 0.5 * (1.0 + th)
        act = v * half_up
        slope = half_up + 0.5 * v * (1.0 - th * th) * (root * (1.0 + 3 * 0.044715 * vv))
        for g in range(group):
            m = n * group + g
            rows_g = slice(g * own, (g + 1) * own)
            res[m] = (xp[m, :own, :].astype(F32) + act[rows_g]).astype(BF)
            gp[m, :own, :] = (og[m].astype(F32) * slope[rows_g]).astype(BF)
        return carry

    lax.fori_loop(0, members // group, forward, 0)
    send(1)

    grad = gp[:, :own, :].reshape(members * own, chan)
    some = basis // chunks
    def mix(n):
        for u in range(some):
            k = n * some + u
            part = lax.dot_general(
                feats[:, k * chan : (k + 1) * chan], grad, (((0,), (0,)), ((), ())),
                preferred_element_type=F32,
            )
            part = (part * scale).astype(wg.dtype)
            for z in range(lons):
                for h in range(2):
                    wg[n, h, z, u * held : (u + 1) * held, :] = part[
                        z * held : (z + 1) * held, h * half : (h + 1) * half
                    ]

    def push(n, src, dst, slot, where):
        one = pltpu.make_async_remote_copy(
            src_ref=src, dst_ref=dst, send_sem=wssem.at[n, slot], recv_sem=wrsem.at[n, slot],
            device_id=where, device_id_type=MESH,
        )
        one.start()
        return one

    own_piece = pl.ds(pl.multiple_of(mine * piece, 16), piece)
    flight = {}

    def to_pair(n):
        flight[n, 0] = [
            push(n, wg.at[n, 1 - core], pair_in.at[n], 0, {"lat": lat + 1 - 2 * core})
        ]

    def arrived(n, stage):
        for one in flight[n, stage]:
            one.wait_recv()

    def to_plane(n):
        arrived(n, 0)

        def add(z, carry):
            wg[n, core, z] = (wg[n, core, z].astype(F32) + pair_in[n, z].astype(F32)).astype(BF)
            return carry

        lax.fori_loop(0, lons, add, 0)
        flight[n, 1] = []
        for hop in range(1, plane):
            where, other = in_plane(hop)
            at = pl.ds(pl.multiple_of(other * piece, 16), piece)
            flight[n, 1].append(
                push(n, wg.at[n, core, :, at, :], plane_in.at[n, hop - 1], hop, where)
            )

    def to_lon(n):
        arrived(n, 1)

        def add(z, carry):
            acc = wg[n, core, z, own_piece, :].astype(F32)
            for hop in range(plane - 1):
                acc = acc + plane_in[n, hop, z].astype(F32)
            plane_sum[n, z] = acc.astype(BF)
            return carry

        lax.fori_loop(0, lons, add, 0)
        flight[n, 2] = []
        for hop in range(1, lons):
            other = lax.rem(lon + hop, lons)
            flight[n, 2].append(
                push(
                    n, plane_sum.at[n, other], lon_in.at[n, hop - 1], plane - 1 + hop,
                    {"lon": other},
                )
            )

    def to_group(n):
        arrived(n, 2)
        acc = plane_sum[n, lon].astype(F32)
        for hop in range(lons - 1):
            acc = acc + lon_in[n, hop].astype(F32)
        done[n, core, own_piece, :] = acc.astype(BF)
        spot = done.at[n, core, own_piece, :]
        flight[n, 3] = [
            push(n, spot, spot, plane + lons - 2 + hop, in_group(hop))
            for hop in range(1, enss * lats)
        ]

    def keep(n):
        arrived(n, 3)
        for h in range(2):
            full = done[n, h].astype(F32)
            for u in range(some):
                share[n * some + u, :, h * half : (h + 1) * half] = full[
                    u * held : (u + 1) * held
                ]

    def backward(n, carry):
        at = pl.ds(pl.multiple_of(n * (group * own), own), group * own)
        acc = None
        for k in range(basis):
            term = lax.dot_general(
                feats[at, k * chan : (k + 1) * chan], w[k], (((1,), (1,)), ((), ())),
                preferred_element_type=F32,
            )
            acc = term if acc is None else acc + term
        for g in range(group):
            m = n * group + g
            ing[m] = (og[m].astype(F32) + acc[g * own : (g + 1) * own]).astype(BF)
        return carry

    for n in range(chunks):
        mix(n)
        to_pair(n)
        if n:
            to_plane(n - 1)
    lax.fori_loop(0, rows, build_adjoint, 0)
    to_plane(chunks - 1)
    receive(1)
    spread_some(adj, gp, 0, members // 2)
    to_lon(0)
    spread_some(adj, gp, members // 2, members)
    for n in range(1, chunks - 1):
        to_lon(n)
    turns = members // group
    lax.fori_loop(0, turns // 2, backward, 0)
    to_group(0)
    lax.fori_loop(turns // 2, turns, backward, 0)
    if chunks > 1:
        to_lon(chunks - 1)
    for n in range(1, chunks):
        to_group(n)
    sent(0)
    sent(1)
    for n in range(chunks):
        keep(n)
    for copies_sent in flight.values():
        for one in copies_sent:
            one.wait_send()


def place_kernel(res_in, ing_in, wg_in, res_out, ing_out, wg_out, sem):
    moves = []
    for src, dst in ((res_in, res_out), (ing_in, ing_out), (wg_in, wg_out)):
        for part in range(src.shape[0]):
            moves.append(
                pltpu.make_async_copy(src.at[part], dst.at[part], sem.at[len(moves)])
            )
    for one in moves:
        one.start()
    for one in moves:
        one.wait()


def shards(members_in, out_grad, weight, basis_blocks, cycle_block, half_width):
    members, rows, cols, chan = members_in.shape
    blocks, basis, reach, taps = basis_blocks.shape
    own = rows * cols
    enss, lats, lons = (lax.axis_size(axis) for axis in ("ens", "lat", "lon"))
    plane = enss * lats // 2
    held = chan // lons
    chunks = 3 if basis % 3 == 0 else 1
    span = -(-(basis // chunks) * held // (16 * plane)) * 16 * plane
    piece = span // plane
    half = chan // 2
    used, depth, pos, select, regroup = layout(members, rows, cols)
    tall = -(-taps // 16) * 16
    cell_count = members * enss * own * lats * lons
    dims = (
        members, rows, cols, chan, basis, used, depth, enss, lats, lons, cycle_block.shape[0],
        1.0 / math.sqrt(cell_count),
    )
    vmem = pl.BlockSpec(memory_space=pltpu.VMEM)
    hbm = pl.BlockSpec(memory_space=pltpu.HBM)
    smem = pl.BlockSpec(memory_space=pltpu.SMEM)
    cells = (members, own, chan)
    padded = (members, depth, chan)
    slots = 6 + 2 * members
    pushes = plane + lons - 1 + enss * lats - 1
    res, ing, weight_grad = pl.pallas_call(
        functools.partial(block_kernel, dims),
        out_shape=[
            pltpu.VMEM(cells, BF),
            pltpu.VMEM(cells, BF),
            pltpu.VMEM((basis, held, chan), F32),
        ],
        in_specs=[hbm] * 4 + [smem, smem] + [hbm] * 3,
        out_specs=[vmem] * 3,
        scratch_shapes=[
            pltpu.VMEM(padded, BF),
            pltpu.VMEM(padded, BF),
            pltpu.VMEM(cells, BF),
            pltpu.VMEM((basis, chan, chan), BF),
            pltpu.VMEM((members * own, basis * chan), BF),
            pltpu.VMEM((basis * own, depth), BF),
            pltpu.VMEM((basis * own, depth), BF),
            pltpu.VMEM((2, members * select.shape[0], chan), BF),
            pltpu.VMEM((2, 4, members * H, chan), BF),
            pltpu.VMEM((chunks, 2, lons, span, half), BF),
            pltpu.VMEM((chunks, lons, span, half), BF),
            pltpu.VMEM((chunks, plane - 1, lons, piece, half), BF),
            pltpu.VMEM((chunks, lons, piece, half), BF),
            pltpu.VMEM((chunks, lons - 1, piece, half), BF),
            pltpu.VMEM((chunks, 2, span, half), BF),
            pltpu.VMEM((basis * tall, reach * blocks), F32),
            pltpu.VMEM((basis, reach, blocks, taps), F32),
            pltpu.VMEM(pos.shape, jnp.int32),
            pltpu.VMEM(select.shape, BF),
            pltpu.VMEM(regroup.shape, BF),
            pltpu.SemaphoreType.DMA((10,)),
            pltpu.SemaphoreType.DMA((2, slots)),
            pltpu.SemaphoreType.DMA((2, slots)),
            pltpu.SemaphoreType.DMA((chunks, pushes)),
            pltpu.SemaphoreType.DMA((chunks, pushes)),
        ],
        compiler_params=pltpu.CompilerParams(
            collective_id=0, has_side_effects=True, vmem_limit_bytes=VMEM
        ),
    )(
        members_in.reshape(cells), out_grad.reshape(cells), weight,
        jnp.transpose(basis_blocks, (1, 2, 0, 3)), cycle_block, half_width.T,
        jnp.asarray(pos), jnp.asarray(select, dtype=BF), jnp.asarray(regroup, dtype=BF),
    )
    held_back = [res, ing, weight_grad]
    res, ing, weight_grad = pl.pallas_call(
        place_kernel,
        out_shape=[jax.ShapeDtypeStruct(a.shape, a.dtype) for a in held_back],
        in_specs=[vmem] * 3,
        out_specs=[hbm] * 3,
        scratch_shapes=[pltpu.SemaphoreType.DMA((sum(a.shape[0] for a in held_back),))],
        compiler_params=pltpu.CompilerParams(vmem_limit_bytes=VMEM // 4),
    )(*held_back)
    return (res.reshape(members_in.shape), ing.reshape(members_in.shape), weight_grad)


def solution(mesh):
    cells = P("ens", "lat", "lon", None)
    return jax.shard_map(
        shards,
        mesh=mesh,
        in_specs=(cells, cells, P(), P(), P(), P()),
        out_specs=(cells, cells, P(None, "lon", None)),
        check_vma=False,
    )
```

```python
import functools
import math

import jax
import jax.numpy as jnp
import numpy as np
from jax import lax
from jax.experimental import pallas as pl
from jax.experimental.pallas import tpu as pltpu
from jax.sharding import PartitionSpec as P

R = 1
H = 4
VMEM = 60 * 1024 * 1024
MESH = pl.DeviceIdType.MESH
BF = jnp.bfloat16
F32 = jnp.float32


def layout(members, rows, cols):
    cells = [(i, j) for i in range(rows) for j in range(cols)]
    cells += [(-1, j) for j in range(cols)] + [(rows, j) for j in range(cols)]
    cells += [(i, j - H) for i in range(rows) for j in range(H)]
    cells += [(i, cols + j) for i in range(rows) for j in range(H)]
    for i in (-1, rows):
        for first in (-H, cols):
            cells += [(i, first + j) for j in range(H)]
    depth = -(-len(cells) // 128) * 128
    pos = np.full((8, depth), -1000, np.int32)
    for p, (i, j) in enumerate(cells):
        pos[0, p], pos[1, p] = i, j
    own = rows * cols
    picks = [i * cols + j for i in range(rows) for j in range(H)]
    picks += [i * cols + cols - H + j for i in range(rows) for j in range(H)]
    picks += [i * cols + f + j for i in (0, rows - 1) for f in (0, cols - H) for j in range(H)]
    select = np.zeros((len(picks), own), np.float32)
    select[np.arange(len(picks)), picks] = 1
    corners = 4 * members * H
    regroup = np.zeros((corners, corners), np.float32)
    for m in range(members):
        for q in range(4):
            for j in range(H):
                regroup[(m * 4 + q) * H + j, (q * members + m) * H + j] = 1
    return len(cells), depth, pos, select, regroup


def block_kernel(
    dims,
    x_hbm, og_hbm, w_hbm, basis_hbm, cb_ref, hw_ref, pos_hbm, select_hbm, regroup_hbm,
    res, ing, share,
    xp, gp, og, w, feats, fwd, adj, packs, crecv, wg, pair_in, plane_in, plane_sum,
    lon_in, done, lines,
    basis_ref, pos_ref, select_ref, regroup_ref, lsem, ssem, rsem, wssem, wrsem,
):
    members, rows, cols, chan, basis, used, depth, enss, lats, lons, total, scale = dims
    own = rows * cols
    rim = rows * H
    taps = 2 * H + 1
    lat = lax.axis_index("lat")
    lon = lax.axis_index("lon")
    west = lax.rem(lon + lons - 1, lons)
    east = lax.rem(lon + 1, lons)
    has_n = lat > 0
    has_s = lat < lats - 1
    ens = lax.axis_index("ens")
    chips = lats // 2
    plane = enss * chips
    core = lax.rem(lat, 2)
    mine = ens * chips + lat // 2
    held = chan // lons
    chunks, span = wg.shape[0], wg.shape[3]
    piece = span // plane
    group = 2 if members % 2 == 0 else 1
    half = chan // 2

    load_x = pltpu.make_async_copy(x_hbm, xp.at[:, pl.ds(0, own), :], lsem.at[0])
    load_x.start()
    loads = [
        pltpu.make_async_copy(src, dst, lsem.at[6 + n])
        for n, (src, dst) in enumerate(
            [
                (select_hbm, select_ref), (regroup_hbm, regroup_ref),
                (basis_hbm, basis_ref), (pos_hbm, pos_ref),
            ]
        )
    ]
    for one in loads:
        one.start()
    load_og = pltpu.make_async_copy(og_hbm, og, lsem.at[1])
    load_og.start()
    load_w = pltpu.make_async_copy(w_hbm, w, lsem.at[2])
    load_w.start()

    barrier = pltpu.get_barrier_semaphore()

    def greet(where):
        pl.semaphore_signal(barrier, inc=1, device_id=where, device_id_type=MESH)

    greet({"lon": west})
    greet({"lon": east})

    def in_plane(step):
        other = lax.rem(mine + step, plane)
        return {"ens": other // chips, "lat": 2 * lax.rem(other, chips) + core}, other

    def in_group(step):
        other = lax.rem(ens * lats + lat + step, enss * lats)
        return {"ens": other // lats, "lat": lax.rem(other, lats)}

    for hop in range(1, enss * lats):
        greet(in_group(hop))
    for hop in range(1, lons):
        greet({"lon": lax.rem(lon + hop, lons)})

    @pl.when(has_n)
    def _():
        for z in (lon, west, east):
            greet({"lat": lat - 1, "lon": z})

    @pl.when(has_s)
    def _():
        for z in (lon, west, east):
            greet({"lat": lat + 1, "lon": z})

    def clear(pad, land):
        pad[:, used:, :] = jnp.zeros((members, depth - used, chan), BF)

        @pl.when(jnp.logical_not(has_n))
        def _():
            pad[:, own : own + cols, :] = jnp.zeros((members, cols, chan), BF)
            land[0:2] = jnp.zeros((2,) + land.shape[1:], BF)

        @pl.when(jnp.logical_not(has_s))
        def _():
            pad[:, own + cols : own + 2 * cols, :] = jnp.zeros((members, cols, chan), BF)
            land[2:4] = jnp.zeros((2,) + land.shape[1:], BF)

    wide = members * rim
    mh = members * H

    def copies(t):
        pad = (xp, gp)[t]
        pack = packs.at[t]
        land = crecv.at[t]
        top, bottom = pl.ds(own, cols), pl.ds(own + cols, cols)
        left, right = pl.ds(own + 2 * cols, rim), pl.ds(own + 2 * cols + rim, rim)
        corner = lambda q: pack.at[pl.ds(2 * wide + q * mh, mh)]
        north, south = {"lat": lat - 1}, {"lat": lat + 1}
        plan = [
            (pad.at[:, pl.ds(0, cols), :], pad.at[:, bottom, :], north),
            (pad.at[:, pl.ds(own - cols, cols), :], pad.at[:, top, :], south),
            (None, right, {"lon": west}),
            (None, left, {"lon": east}),
            (corner(0), land.at[3], {"lat": lat - 1, "lon": west}),
            (corner(1), land.at[2], {"lat": lat - 1, "lon": east}),
            (corner(2), land.at[1], {"lat": lat + 1, "lon": west}),
            (corner(3), land.at[0], {"lat": lat + 1, "lon": east}),
        ]
        out = {}
        slot = 0
        for q, (src, dst, where) in enumerate(plan):
            if src is None:
                parts = [
                    (pack.at[pl.ds((q - 2) * wide + m * rim, rim)], pad.at[m, dst, :])
                    for m in range(members)
                ]
            else:
                parts = [(src, dst)]
            out[q] = []
            for a, b in parts:
                out[q].append(
                    pltpu.make_async_remote_copy(
                        src_ref=a, dst_ref=b, send_sem=ssem.at[t, slot], recv_sem=rsem.at[t, slot],
                        device_id=where, device_id_type=MESH,
                    )
                )
                slot += 1
        return out

    NORTH, SOUTH, SIDES = (0, 4, 5), (1, 6, 7), (2, 3)

    def each(c, qs, act):
        for q in qs:
            for one in c[q]:
                act(one)

    def send(t):
        c = copies(t)
        pad = (xp, gp)[t]

        ends = []
        for m in range(members):
            got = jnp.dot(
                select_ref[...], pad[m, :own, :], preferred_element_type=F32
            )
            packs[t, m * rim : (m + 1) * rim] = got[:rim].astype(BF)
            packs[t, wide + m * rim : wide + (m + 1) * rim] = got[rim : 2 * rim].astype(BF)
            ends.append(got[2 * rim :])
        packs[t, 2 * wide :] = lax.dot_general(
            regroup_ref[...], jnp.concatenate(ends, 0).astype(BF), (((0,), (0,)), ((), ())),
            preferred_element_type=F32,
        ).astype(BF)
        each(c, SIDES, lambda one: one.start())

        @pl.when(has_n)
        def _():
            each(c, NORTH, lambda one: one.start())

        @pl.when(has_s)
        def _():
            each(c, SOUTH, lambda one: one.start())

    def receive(t):
        c = copies(t)
        pad = (xp, gp)[t]

        each(c, SIDES, lambda one: one.wait_recv())

        @pl.when(has_s)
        def _():
            each(c, NORTH, lambda one: one.wait_recv())

        @pl.when(has_n)
        def _():
            each(c, SOUTH, lambda one: one.wait_recv())

        got = jnp.dot(
            regroup_ref[...], crecv[t].reshape(4 * mh, chan), preferred_element_type=F32
        ).astype(BF)
        for m in range(members):
            pad[m, used - 4 * H : used, :] = got[m * 4 * H : (m + 1) * 4 * H]

    def sent(t):
        c = copies(t)
        each(c, SIDES, lambda one: one.wait_send())

        @pl.when(has_n)
        def _():
            each(c, NORTH, lambda one: one.wait_send())

        @pl.when(has_s)
        def _():
            each(c, SOUTH, lambda one: one.wait_send())

    clear(xp, crecv.at[0])
    clear(gp, crecv.at[1])
    load_x.wait()
    for one in loads:
        one.wait()
    pl.semaphore_wait(
        barrier,
        lons + enss * lats + 3 * has_n.astype(jnp.int32) + 3 * has_s.astype(jnp.int32),
    )
    send(0)

    blocks = basis_ref.shape[2]
    sides = 2 * R + 1
    tall = lines.shape[0] // basis
    eye = (
        lax.broadcasted_iota(jnp.int32, (tall, taps), 0)
        == lax.broadcasted_iota(jnp.int32, (tall, taps), 1)
    ).astype(F32).astype(BF)
    for k in range(basis):
        entries = basis_ref[k].reshape(sides * blocks, taps).astype(BF)
        lines[k * tall : (k + 1) * tall, :] = lax.dot_general(
            eye, entries, (((1,), (1,)), ((), ())), preferred_element_type=F32
        )
    lane = lax.broadcasted_iota(jnp.int32, lines.shape, 1)
    far = jnp.abs(lax.broadcasted_iota(jnp.int32, lines.shape, 0) % tall - H)
    first = lat * rows
    cell_i, cell_j = pos_ref[0:1, :], pos_ref[1:2, :]
    entry = lax.broadcasted_iota(jnp.int32, (sides * blocks, depth), 0)
    offset = entry // blocks
    which = entry % blocks
    col = lax.broadcasted_iota(jnp.int32, (cols, depth), 0)
    ahead = cell_j - col + H
    behind = col - cell_j + H

    def by_side(index, values):
        return jnp.where(index == 0, values[0], jnp.where(index == 1, values[1], values[2]))

    def expand(cycles, wanted, tap, dst, i):
        cycles = [jnp.clip(first + cyc, 0, total - 1) for cyc in cycles]
        span = by_side(lane // blocks, [hw_ref[r, cyc] for r, cyc in enumerate(cycles)])
        table = jnp.where(far <= span, lines[...], 0.0).astype(BF)
        block = by_side(offset, [cb_ref[cyc] for cyc in cycles])
        hit = jnp.logical_and(wanted == offset, which == block)
        spread = jnp.dot(
            table, jnp.where(hit, 1.0, 0.0).astype(BF), preferred_element_type=F32
        )
        for k in range(basis):
            acc = jnp.zeros((cols, depth), F32)
            for d in range(taps):
                line = spread[k * tall + d : k * tall + d + 1, :]
                acc = jnp.where(tap == d, line, acc)
            dst[pl.ds(pl.multiple_of(k * own + i * cols, cols), cols), :] = acc.astype(BF)

    def build_forward(i, carry):
        expand([i] * sides, cell_i - i + R, ahead, fwd, i)
        return carry

    def build_adjoint(i, carry):
        expand([i + R - r for r in range(sides)], i + R - cell_i, behind, adj, i)
        return carry

    lax.fori_loop(0, rows, build_forward, 0, unroll=4 if rows % 4 == 0 else 1)

    def spread_some(mat, pad, begin, end):
        def one(m, carry):
            block = pad[m]
            at = pl.ds(pl.multiple_of(m * own, own), own)
            for k in range(basis):
                feats[at, k * chan : (k + 1) * chan] = jnp.dot(
                    mat[k * own : (k + 1) * own, :], block, preferred_element_type=F32
                ).astype(BF)
            return carry

        lax.fori_loop(begin, end, one, 0, unroll=True)

    receive(0)
    spread_some(fwd, xp, 0, members)
    load_w.wait()
    load_og.wait()

    def forward(n, carry):
        at = pl.ds(pl.multiple_of(n * (group * own), own), group * own)
        v = jnp.dot(
            feats[at, :], w[...].reshape(basis * chan, chan), preferred_element_type=F32
        )
        root = math.sqrt(2.0 / math.pi)
        vv = v * v
        th = jnp.tanh(root * (v + 0.044715 * (vv * v)))
        half_up = 0.5 * (1.0 + th)
        act = v * half_up
        slope = half_up + 0.5 * v * (1.0 - th * th) * (root * (1.0 + 3 * 0.044715 * vv))
        for g in range(group):
            m = n * group + g
            rows_g = slice(g * own, (g + 1) * own)
            res[m] = (xp[m, :own, :].astype(F32) + act[rows_g]).astype(BF)
            gp[m, :own, :] = (og[m].astype(F32) * slope[rows_g]).astype(BF)
        return carry

    lax.fori_loop(0, members // group, forward, 0, unroll=True)
    send(1)

    grad = gp[:, :own, :].reshape(members * own, chan)
    some = basis // chunks
    def mix(n):
        for u in range(some):
            k = n * some + u
            part = lax.dot_general(
                feats[:, k * chan : (k + 1) * chan], grad, (((0,), (0,)), ((), ())),
                preferred_element_type=F32,
            )
            part = (part * scale).astype(wg.dtype)
            for z in range(lons):
                for h in range(2):
                    wg[n, h, z, u * held : (u + 1) * held, :] = part[
                        z * held : (z + 1) * held, h * half : (h + 1) * half
                    ]

    def push(n, src, dst, slot, where):
        one = pltpu.make_async_remote_copy(
            src_ref=src, dst_ref=dst, send_sem=wssem.at[n, slot], recv_sem=wrsem.at[n, slot],
            device_id=where, device_id_type=MESH,
        )
        one.start()
        return one

    own_piece = pl.ds(pl.multiple_of(mine * piece, 16), piece)
    flight = {}

    def to_pair(n):
        flight[n, 0] = [
            push(n, wg.at[n, 1 - core], pair_in.at[n], 0, {"lat": lat + 1 - 2 * core})
        ]

    def arrived(n, stage):
        for one in flight[n, stage]:
            one.wait_recv()

    def to_plane(n):
        arrived(n, 0)

        def add(z, carry):
            wg[n, core, z] = (wg[n, core, z].astype(F32) + pair_in[n, z].astype(F32)).astype(BF)
            return carry

        lax.fori_loop(0, lons, add, 0)
        flight[n, 1] = []
        for hop in range(1, plane):
            where, other = in_plane(hop)
            at = pl.ds(pl.multiple_of(other * piece, 16), piece)
            flight[n, 1].append(
                push(n, wg.at[n, core, :, at, :], plane_in.at[n, hop - 1], hop, where)
            )

    def to_lon(n):
        arrived(n, 1)

        def add(z, carry):
            acc = wg[n, core, z, own_piece, :].astype(F32)
            for hop in range(plane - 1):
                acc = acc + plane_in[n, hop, z].astype(F32)
            plane_sum[n, z] = acc.astype(BF)
            return carry

        lax.fori_loop(0, lons, add, 0)
        flight[n, 2] = []
        for hop in range(1, lons):
            other = lax.rem(lon + hop, lons)
            flight[n, 2].append(
                push(
                    n, plane_sum.at[n, other], lon_in.at[n, hop - 1], plane - 1 + hop,
                    {"lon": other},
                )
            )

    def to_group(n):
        arrived(n, 2)
        acc = plane_sum[n, lon].astype(F32)
        for hop in range(lons - 1):
            acc = acc + lon_in[n, hop].astype(F32)
        done[n, core, own_piece, :] = acc.astype(BF)
        spot = done.at[n, core, own_piece, :]
        flight[n, 3] = [
            push(n, spot, spot, plane + lons - 2 + hop, in_group(hop))
            for hop in range(1, enss * lats)
        ]

    def keep(n):
        arrived(n, 3)
        for h in range(2):
            full = done[n, h].astype(F32)
            for u in range(some):
                share[n * some + u, :, h * half : (h + 1) * half] = full[
                    u * held : (u + 1) * held
                ]

    def backward(n, carry):
        at = pl.ds(pl.multiple_of(n * (group * own), own), group * own)
        acc = None
        for k in range(basis):
            term = lax.dot_general(
                feats[at, k * chan : (k + 1) * chan], w[k], (((1,), (1,)), ((), ())),
                preferred_element_type=F32,
            )
            acc = term if acc is None else acc + term
        for g in range(group):
            m = n * group + g
            ing[m] = (og[m].astype(F32) + acc[g * own : (g + 1) * own]).astype(BF)
        return carry

    for n in range(chunks):
        mix(n)
        to_pair(n)
        if n:
            to_plane(n - 1)
    lax.fori_loop(0, rows, build_adjoint, 0, unroll=4 if rows % 4 == 0 else 1)
    to_plane(chunks - 1)
    receive(1)
    spread_some(adj, gp, 0, members // 2)
    to_lon(0)
    spread_some(adj, gp, members // 2, members)
    for n in range(1, chunks - 1):
        to_lon(n)
    turns = members // group
    lax.fori_loop(0, turns // 2, backward, 0)
    to_group(0)
    lax.fori_loop(turns // 2, turns, backward, 0)
    if chunks > 1:
        to_lon(chunks - 1)
    for n in range(1, chunks):
        to_group(n)
    sent(0)
    sent(1)
    for n in range(chunks):
        keep(n)
    for copies_sent in flight.values():
        for one in copies_sent:
            one.wait_send()


def place_kernel(res_in, ing_in, wg_in, res_out, ing_out, wg_out, sem):
    moves = []
    for src, dst in ((res_in, res_out), (ing_in, ing_out), (wg_in, wg_out)):
        for part in range(src.shape[0]):
            moves.append(
                pltpu.make_async_copy(src.at[part], dst.at[part], sem.at[len(moves)])
            )
    for one in moves:
        one.start()
    for one in moves:
        one.wait()


def shards(members_in, out_grad, weight, basis_blocks, cycle_block, half_width):
    members, rows, cols, chan = members_in.shape
    blocks, basis, reach, taps = basis_blocks.shape
    own = rows * cols
    enss, lats, lons = (lax.axis_size(axis) for axis in ("ens", "lat", "lon"))
    plane = enss * lats // 2
    held = chan // lons
    chunks = 3 if basis % 3 == 0 else 1
    span = -(-(basis // chunks) * held // (16 * plane)) * 16 * plane
    piece = span // plane
    half = chan // 2
    used, depth, pos, select, regroup = layout(members, rows, cols)
    tall = -(-taps // 16) * 16
    cell_count = members * enss * own * lats * lons
    dims = (
        members, rows, cols, chan, basis, used, depth, enss, lats, lons, cycle_block.shape[0],
        1.0 / math.sqrt(cell_count),
    )
    vmem = pl.BlockSpec(memory_space=pltpu.VMEM)
    hbm = pl.BlockSpec(memory_space=pltpu.HBM)
    smem = pl.BlockSpec(memory_space=pltpu.SMEM)
    cells = (members, own, chan)
    padded = (members, depth, chan)
    slots = 6 + 2 * members
    pushes = plane + lons - 1 + enss * lats - 1
    res, ing, weight_grad = pl.pallas_call(
        functools.partial(block_kernel, dims),
        out_shape=[
            pltpu.VMEM(cells, BF),
            pltpu.VMEM(cells, BF),
            pltpu.VMEM((basis, held, chan), F32),
        ],
        in_specs=[hbm] * 4 + [smem, smem] + [hbm] * 3,
        out_specs=[vmem] * 3,
        scratch_shapes=[
            pltpu.VMEM(padded, BF),
            pltpu.VMEM(padded, BF),
            pltpu.VMEM(cells, BF),
            pltpu.VMEM((basis, chan, chan), BF),
            pltpu.VMEM((members * own, basis * chan), BF),
            pltpu.VMEM((basis * own, depth), BF),
            pltpu.VMEM((basis * own, depth), BF),
            pltpu.VMEM((2, members * select.shape[0], chan), BF),
            pltpu.VMEM((2, 4, members * H, chan), BF),
            pltpu.VMEM((chunks, 2, lons, span, half), BF),
            pltpu.VMEM((chunks, lons, span, half), BF),
            pltpu.VMEM((chunks, plane - 1, lons, piece, half), BF),
            pltpu.VMEM((chunks, lons, piece, half), BF),
            pltpu.VMEM((chunks, lons - 1, piece, half), BF),
            pltpu.VMEM((chunks, 2, span, half), BF),
            pltpu.VMEM((basis * tall, reach * blocks), F32),
            pltpu.VMEM((basis, reach, blocks, taps), F32),
            pltpu.VMEM(pos.shape, jnp.int32),
            pltpu.VMEM(select.shape, BF),
            pltpu.VMEM(regroup.shape, BF),
            pltpu.SemaphoreType.DMA((10,)),
            pltpu.SemaphoreType.DMA((2, slots)),
            pltpu.SemaphoreType.DMA((2, slots)),
            pltpu.SemaphoreType.DMA((chunks, pushes)),
            pltpu.SemaphoreType.DMA((chunks, pushes)),
        ],
        compiler_params=pltpu.CompilerParams(
            collective_id=0, has_side_effects=True, vmem_limit_bytes=VMEM
        ),
    )(
        members_in.reshape(cells), out_grad.reshape(cells), weight,
        jnp.transpose(basis_blocks, (1, 2, 0, 3)), cycle_block, half_width.T,
        jnp.asarray(pos), jnp.asarray(select, dtype=BF), jnp.asarray(regroup, dtype=BF),
    )
    held_back = [res, ing, weight_grad]
    res, ing, weight_grad = pl.pallas_call(
        place_kernel,
        out_shape=[jax.ShapeDtypeStruct(a.shape, a.dtype) for a in held_back],
        in_specs=[vmem] * 3,
        out_specs=[hbm] * 3,
        scratch_shapes=[pltpu.SemaphoreType.DMA((sum(a.shape[0] for a in held_back),))],
        compiler_params=pltpu.CompilerParams(vmem_limit_bytes=VMEM // 4),
    )(*held_back)
    return (res.reshape(members_in.shape), ing.reshape(members_in.shape), weight_grad)


def solution(mesh):
    cells = P("ens", "lat", "lon", None)
    return jax.shard_map(
        shards,
        mesh=mesh,
        in_specs=(cells, cells, P(), P(), P(), P()),
        out_specs=(cells, cells, P(None, "lon", None)),
        check_vma=False,
    )
```

```python
import functools
import math

import jax
import jax.numpy as jnp
import numpy as np
from jax import lax
from jax.experimental import pallas as pl
from jax.experimental.pallas import tpu as pltpu
from jax.sharding import PartitionSpec as P

R = 1
H = 4
VMEM = 60 * 1024 * 1024
MESH = pl.DeviceIdType.MESH
BF = jnp.bfloat16
F32 = jnp.float32


def layout(members, rows, cols):
    cells = [(i, j) for i in range(rows) for j in range(cols)]
    cells += [(-1, j) for j in range(cols)] + [(rows, j) for j in range(cols)]
    cells += [(i, j - H) for i in range(rows) for j in range(H)]
    cells += [(i, cols + j) for i in range(rows) for j in range(H)]
    for i in (-1, rows):
        for first in (-H, cols):
            cells += [(i, first + j) for j in range(H)]
    depth = -(-len(cells) // 128) * 128
    pos = np.full((8, depth), -1000, np.int32)
    for p, (i, j) in enumerate(cells):
        pos[0, p], pos[1, p] = i, j
    own = rows * cols
    picks = [i * cols + j for i in range(rows) for j in range(H)]
    picks += [i * cols + cols - H + j for i in range(rows) for j in range(H)]
    picks += [i * cols + f + j for i in (0, rows - 1) for f in (0, cols - H) for j in range(H)]
    select = np.zeros((len(picks), own), np.float32)
    select[np.arange(len(picks)), picks] = 1
    corners = 4 * members * H
    regroup = np.zeros((corners, corners), np.float32)
    for m in range(members):
        for q in range(4):
            for j in range(H):
                regroup[(m * 4 + q) * H + j, (q * members + m) * H + j] = 1
    return len(cells), depth, pos, select, regroup


def block_kernel(
    dims,
    x_hbm, og_hbm, w_hbm, basis_hbm, cb_ref, hw_ref, pos_hbm, select_hbm, regroup_hbm,
    res, ing, share,
    xp, gp, og, w, feats, fwd, adj, packs, crecv, wg, pair_in, plane_in, plane_sum,
    lon_in, done, lon_wide, wide_sum, lines,
    basis_ref, pos_ref, select_ref, regroup_ref, lsem, ssem, rsem, wssem, wrsem,
):
    members, rows, cols, chan, basis, used, depth, enss, lats, lons, total, scale = dims
    own = rows * cols
    rim = rows * H
    taps = 2 * H + 1
    lat = lax.axis_index("lat")
    lon = lax.axis_index("lon")
    west = lax.rem(lon + lons - 1, lons)
    east = lax.rem(lon + 1, lons)
    has_n = lat > 0
    has_s = lat < lats - 1
    ens = lax.axis_index("ens")
    chips = lats // 2
    plane = enss * chips
    core = lax.rem(lat, 2)
    mine = ens * chips + lat // 2
    held = chan // lons
    chunks, span = wg.shape[0], wg.shape[3]
    piece = span // plane
    group = 2 if members % 2 == 0 else 1
    half = chan // 2

    load_x = pltpu.make_async_copy(x_hbm, xp.at[:, pl.ds(0, own), :], lsem.at[0])
    load_x.start()
    loads = [
        pltpu.make_async_copy(src, dst, lsem.at[6 + n])
        for n, (src, dst) in enumerate(
            [
                (select_hbm, select_ref), (regroup_hbm, regroup_ref),
                (basis_hbm, basis_ref), (pos_hbm, pos_ref),
            ]
        )
    ]
    for one in loads:
        one.start()
    load_og = pltpu.make_async_copy(og_hbm, og, lsem.at[1])
    load_og.start()
    load_w = pltpu.make_async_copy(w_hbm, w, lsem.at[2])
    load_w.start()

    barrier = pltpu.get_barrier_semaphore()

    def greet(where):
        pl.semaphore_signal(barrier, inc=1, device_id=where, device_id_type=MESH)

    greet({"lon": west})
    greet({"lon": east})

    def in_plane(step):
        other = lax.rem(mine + step, plane)
        return {"ens": other // chips, "lat": 2 * lax.rem(other, chips) + core}, other

    def in_group(step):
        other = lax.rem(ens * lats + lat + step, enss * lats)
        return {"ens": other // lats, "lat": lax.rem(other, lats)}

    for hop in range(1, enss * lats):
        greet(in_group(hop))
    for hop in range(1, lons):
        greet({"lon": lax.rem(lon + hop, lons)})

    @pl.when(has_n)
    def _():
        for z in (lon, west, east):
            greet({"lat": lat - 1, "lon": z})

    @pl.when(has_s)
    def _():
        for z in (lon, west, east):
            greet({"lat": lat + 1, "lon": z})

    def clear(pad, land):
        pad[:, used:, :] = jnp.zeros((members, depth - used, chan), BF)

        @pl.when(jnp.logical_not(has_n))
        def _():
            pad[:, own : own + cols, :] = jnp.zeros((members, cols, chan), BF)
            land[0:2] = jnp.zeros((2,) + land.shape[1:], BF)

        @pl.when(jnp.logical_not(has_s))
        def _():
            pad[:, own + cols : own + 2 * cols, :] = jnp.zeros((members, cols, chan), BF)
            land[2:4] = jnp.zeros((2,) + land.shape[1:], BF)

    wide = members * rim
    mh = members * H

    def copies(t):
        pad = (xp, gp)[t]
        pack = packs.at[t]
        land = crecv.at[t]
        top, bottom = pl.ds(own, cols), pl.ds(own + cols, cols)
        left, right = pl.ds(own + 2 * cols, rim), pl.ds(own + 2 * cols + rim, rim)
        corner = lambda q: pack.at[pl.ds(2 * wide + q * mh, mh)]
        north, south = {"lat": lat - 1}, {"lat": lat + 1}
        plan = [
            (pad.at[:, pl.ds(0, cols), :], pad.at[:, bottom, :], north),
            (pad.at[:, pl.ds(own - cols, cols), :], pad.at[:, top, :], south),
            (None, right, {"lon": west}),
            (None, left, {"lon": east}),
            (corner(0), land.at[3], {"lat": lat - 1, "lon": west}),
            (corner(1), land.at[2], {"lat": lat - 1, "lon": east}),
            (corner(2), land.at[1], {"lat": lat + 1, "lon": west}),
            (corner(3), land.at[0], {"lat": lat + 1, "lon": east}),
        ]
        out = {}
        slot = 0
        for q, (src, dst, where) in enumerate(plan):
            if src is None:
                parts = [
                    (pack.at[pl.ds((q - 2) * wide + m * rim, rim)], pad.at[m, dst, :])
                    for m in range(members)
                ]
            else:
                parts = [(src, dst)]
            out[q] = []
            for a, b in parts:
                out[q].append(
                    pltpu.make_async_remote_copy(
                        src_ref=a, dst_ref=b, send_sem=ssem.at[t, slot], recv_sem=rsem.at[t, slot],
                        device_id=where, device_id_type=MESH,
                    )
                )
                slot += 1
        return out

    NORTH, SOUTH, SIDES = (0, 4, 5), (1, 6, 7), (2, 3)

    def each(c, qs, act):
        for q in qs:
            for one in c[q]:
                act(one)

    def send(t):
        c = copies(t)
        pad = (xp, gp)[t]

        ends = []
        for m in range(members):
            got = jnp.dot(
                select_ref[...], pad[m, :own, :], preferred_element_type=F32
            )
            packs[t, m * rim : (m + 1) * rim] = got[:rim].astype(BF)
            packs[t, wide + m * rim : wide + (m + 1) * rim] = got[rim : 2 * rim].astype(BF)
            ends.append(got[2 * rim :])
        packs[t, 2 * wide :] = lax.dot_general(
            regroup_ref[...], jnp.concatenate(ends, 0).astype(BF), (((0,), (0,)), ((), ())),
            preferred_element_type=F32,
        ).astype(BF)
        each(c, SIDES, lambda one: one.start())

        @pl.when(has_n)
        def _():
            each(c, NORTH, lambda one: one.start())

        @pl.when(has_s)
        def _():
            each(c, SOUTH, lambda one: one.start())

    def receive(t):
        c = copies(t)
        pad = (xp, gp)[t]

        each(c, SIDES, lambda one: one.wait_recv())

        @pl.when(has_s)
        def _():
            each(c, NORTH, lambda one: one.wait_recv())

        @pl.when(has_n)
        def _():
            each(c, SOUTH, lambda one: one.wait_recv())

        got = jnp.dot(
            regroup_ref[...], crecv[t].reshape(4 * mh, chan), preferred_element_type=F32
        ).astype(BF)
        for m in range(members):
            pad[m, used - 4 * H : used, :] = got[m * 4 * H : (m + 1) * 4 * H]

    def sent(t):
        c = copies(t)
        each(c, SIDES, lambda one: one.wait_send())

        @pl.when(has_n)
        def _():
            each(c, NORTH, lambda one: one.wait_send())

        @pl.when(has_s)
        def _():
            each(c, SOUTH, lambda one: one.wait_send())

    clear(xp, crecv.at[0])
    clear(gp, crecv.at[1])
    load_x.wait()
    for one in loads:
        one.wait()
    pl.semaphore_wait(
        barrier,
        lons + enss * lats + 3 * has_n.astype(jnp.int32) + 3 * has_s.astype(jnp.int32),
    )
    send(0)

    blocks = basis_ref.shape[2]
    sides = 2 * R + 1
    tall = lines.shape[0] // basis
    eye = (
        lax.broadcasted_iota(jnp.int32, (tall, taps), 0)
        == lax.broadcasted_iota(jnp.int32, (tall, taps), 1)
    ).astype(F32).astype(BF)
    for k in range(basis):
        entries = basis_ref[k].reshape(sides * blocks, taps).astype(BF)
        lines[k * tall : (k + 1) * tall, :] = lax.dot_general(
            eye, entries, (((1,), (1,)), ((), ())), preferred_element_type=F32
        )
    lane = lax.broadcasted_iota(jnp.int32, lines.shape, 1)
    far = jnp.abs(lax.broadcasted_iota(jnp.int32, lines.shape, 0) % tall - H)
    first = lat * rows
    cell_i, cell_j = pos_ref[0:1, :], pos_ref[1:2, :]
    entry = lax.broadcasted_iota(jnp.int32, (sides * blocks, depth), 0)
    offset = entry // blocks
    which = entry % blocks
    col = lax.broadcasted_iota(jnp.int32, (cols, depth), 0)
    ahead = cell_j - col + H
    behind = col - cell_j + H

    def by_side(index, values):
        return jnp.where(index == 0, values[0], jnp.where(index == 1, values[1], values[2]))

    def expand(cycles, wanted, tap, dst, i):
        cycles = [jnp.clip(first + cyc, 0, total - 1) for cyc in cycles]
        span = by_side(lane // blocks, [hw_ref[r, cyc] for r, cyc in enumerate(cycles)])
        table = jnp.where(far <= span, lines[...], 0.0).astype(BF)
        block = by_side(offset, [cb_ref[cyc] for cyc in cycles])
        hit = jnp.logical_and(wanted == offset, which == block)
        spread = jnp.dot(
            table, jnp.where(hit, 1.0, 0.0).astype(BF), preferred_element_type=F32
        )
        for k in range(basis):
            acc = jnp.zeros((cols, depth), F32)
            for d in range(taps):
                line = spread[k * tall + d : k * tall + d + 1, :]
                acc = jnp.where(tap == d, line, acc)
            dst[pl.ds(pl.multiple_of(k * own + i * cols, cols), cols), :] = acc.astype(BF)

    def build_forward(i, carry):
        expand([i] * sides, cell_i - i + R, ahead, fwd, i)
        return carry

    def build_adjoint(i, carry):
        expand([i + R - r for r in range(sides)], i + R - cell_i, behind, adj, i)
        return carry

    lax.fori_loop(0, rows, build_forward, 0, unroll=4 if rows % 4 == 0 else 1)

    def spread_some(mat, pad, begin, end):
        def one(m, carry):
            block = pad[m]
            at = pl.ds(pl.multiple_of(m * own, own), own)
            for k in range(basis):
                feats[at, k * chan : (k + 1) * chan] = jnp.dot(
                    mat[k * own : (k + 1) * own, :], block, preferred_element_type=F32
                ).astype(BF)
            return carry

        lax.fori_loop(begin, end, one, 0, unroll=True)

    receive(0)
    spread_some(fwd, xp, 0, members)
    load_w.wait()
    load_og.wait()

    def forward(n, carry):
        at = pl.ds(pl.multiple_of(n * (group * own), own), group * own)
        v = jnp.dot(
            feats[at, :], w[...].reshape(basis * chan, chan), preferred_element_type=F32
        )
        root = math.sqrt(2.0 / math.pi)
        vv = v * v
        th = jnp.tanh(root * (v + 0.044715 * (vv * v)))
        half_up = 0.5 * (1.0 + th)
        act = v * half_up
        slope = half_up + 0.5 * v * (1.0 - th * th) * (root * (1.0 + 3 * 0.044715 * vv))
        for g in range(group):
            m = n * group + g
            rows_g = slice(g * own, (g + 1) * own)
            res[m] = (xp[m, :own, :].astype(F32) + act[rows_g]).astype(BF)
            gp[m, :own, :] = (og[m].astype(F32) * slope[rows_g]).astype(BF)
        return carry

    lax.fori_loop(0, members // group, forward, 0, unroll=True)
    send(1)

    grad = gp[:, :own, :].reshape(members * own, chan)
    some = basis // chunks
    def mix(n):
        for u in range(some):
            k = n * some + u
            part = lax.dot_general(
                feats[:, k * chan : (k + 1) * chan], grad, (((0,), (0,)), ((), ())),
                preferred_element_type=F32,
            )
            part = (part * scale).astype(wg.dtype)
            for z in range(lons):
                for h in range(2):
                    wg[n, h, z, u * held : (u + 1) * held, :] = part[
                        z * held : (z + 1) * held, h * half : (h + 1) * half
                    ]

    def push(n, src, dst, slot, where):
        one = pltpu.make_async_remote_copy(
            src_ref=src, dst_ref=dst, send_sem=wssem.at[n, slot], recv_sem=wrsem.at[n, slot],
            device_id=where, device_id_type=MESH,
        )
        one.start()
        return one

    own_piece = pl.ds(pl.multiple_of(mine * piece, 16), piece)
    flight = {}

    def to_pair(n):
        flight[n, 0] = [
            push(n, wg.at[n, 1 - core], pair_in.at[n], 0, {"lat": lat + 1 - 2 * core})
        ]

    def arrived(n, stage):
        for one in flight[n, stage]:
            one.wait_recv()

    def add_pair(n):
        arrived(n, 0)

        def add(z, carry):
            wg[n, core, z] = (wg[n, core, z].astype(F32) + pair_in[n, z].astype(F32)).astype(BF)
            return carry

        lax.fori_loop(0, lons, add, 0)

    def lon_before_plane(n):
        add_pair(n)
        flight[n, 2] = []
        for hop in range(1, lons):
            other = lax.rem(lon + hop, lons)
            flight[n, 2].append(
                push(
                    n, wg.at[n, core, other], lon_wide.at[hop - 1], plane - 1 + hop,
                    {"lon": other},
                )
            )

    def plane_after_lon(n):
        arrived(n, 2)
        acc = wg[n, core, lon].astype(F32)
        for hop in range(lons - 1):
            acc = acc + lon_wide[hop].astype(F32)
        wide_sum[...] = acc.astype(BF)
        flight[n, 1] = []
        for hop in range(1, plane):
            where, other = in_plane(hop)
            at = pl.ds(pl.multiple_of(other * piece, 16), piece)
            flight[n, 1].append(
                push(n, wide_sum.at[at, :], plane_in.at[n, hop - 1, 0], hop, where)
            )

    def to_plane(n):
        add_pair(n)
        flight[n, 1] = []
        for hop in range(1, plane):
            where, other = in_plane(hop)
            at = pl.ds(pl.multiple_of(other * piece, 16), piece)
            flight[n, 1].append(
                push(n, wg.at[n, core, :, at, :], plane_in.at[n, hop - 1], hop, where)
            )

    def to_lon(n):
        arrived(n, 1)

        def add(z, carry):
            acc = wg[n, core, z, own_piece, :].astype(F32)
            for hop in range(plane - 1):
                acc = acc + plane_in[n, hop, z].astype(F32)
            plane_sum[n, z] = acc.astype(BF)
            return carry

        lax.fori_loop(0, lons, add, 0)
        flight[n, 2] = []
        for hop in range(1, lons):
            other = lax.rem(lon + hop, lons)
            flight[n, 2].append(
                push(
                    n, plane_sum.at[n, other], lon_in.at[n, hop - 1], plane - 1 + hop,
                    {"lon": other},
                )
            )

    def to_group(n):
        if n == 0:
            arrived(n, 1)
            acc = wide_sum[own_piece, :].astype(F32)
            for hop in range(plane - 1):
                acc = acc + plane_in[n, hop, 0].astype(F32)
        else:
            arrived(n, 2)
            acc = plane_sum[n, lon].astype(F32)
            for hop in range(lons - 1):
                acc = acc + lon_in[n, hop].astype(F32)
        done[n, core, own_piece, :] = acc.astype(BF)
        spot = done.at[n, core, own_piece, :]
        flight[n, 3] = [
            push(n, spot, spot, plane + lons - 2 + hop, in_group(hop))
            for hop in range(1, enss * lats)
        ]

    def keep(n):
        arrived(n, 3)
        for h in range(2):
            full = done[n, h].astype(F32)
            for u in range(some):
                share[n * some + u, :, h * half : (h + 1) * half] = full[
                    u * held : (u + 1) * held
                ]

    def backward(n, carry):
        at = pl.ds(pl.multiple_of(n * (group * own), own), group * own)
        acc = None
        for k in range(basis):
            term = lax.dot_general(
                feats[at, k * chan : (k + 1) * chan], w[k], (((1,), (1,)), ((), ())),
                preferred_element_type=F32,
            )
            acc = term if acc is None else acc + term
        for g in range(group):
            m = n * group + g
            ing[m] = (og[m].astype(F32) + acc[g * own : (g + 1) * own]).astype(BF)
        return carry

    for n in range(chunks):
        mix(n)
        to_pair(n)
        if n == 1:
            lon_before_plane(0)
        if n > 1:
            to_plane(n - 1)
    lax.fori_loop(0, rows, build_adjoint, 0, unroll=4 if rows % 4 == 0 else 1)
    if chunks > 1:
        to_plane(chunks - 1)
    else:
        lon_before_plane(0)
    receive(1)
    spread_some(adj, gp, 0, members // 2)
    plane_after_lon(0)
    spread_some(adj, gp, members // 2, members)
    for n in range(1, chunks - 1):
        to_lon(n)
    turns = members // group
    lax.fori_loop(0, turns // 2, backward, 0)
    to_group(0)
    lax.fori_loop(turns // 2, turns, backward, 0)
    if chunks > 1:
        to_lon(chunks - 1)
    for n in range(1, chunks):
        to_group(n)
    sent(0)
    sent(1)
    for n in range(chunks):
        keep(n)
    for copies_sent in flight.values():
        for one in copies_sent:
            one.wait_send()


def place_kernel(res_in, ing_in, wg_in, res_out, ing_out, wg_out, sem):
    moves = []
    for src, dst in ((res_in, res_out), (ing_in, ing_out), (wg_in, wg_out)):
        for part in range(src.shape[0]):
            moves.append(
                pltpu.make_async_copy(src.at[part], dst.at[part], sem.at[len(moves)])
            )
    for one in moves:
        one.start()
    for one in moves:
        one.wait()


def shards(members_in, out_grad, weight, basis_blocks, cycle_block, half_width):
    members, rows, cols, chan = members_in.shape
    blocks, basis, reach, taps = basis_blocks.shape
    own = rows * cols
    enss, lats, lons = (lax.axis_size(axis) for axis in ("ens", "lat", "lon"))
    plane = enss * lats // 2
    held = chan // lons
    chunks = 3 if basis % 3 == 0 else 1
    span = -(-(basis // chunks) * held // (16 * plane)) * 16 * plane
    piece = span // plane
    half = chan // 2
    used, depth, pos, select, regroup = layout(members, rows, cols)
    tall = -(-taps // 16) * 16
    cell_count = members * enss * own * lats * lons
    dims = (
        members, rows, cols, chan, basis, used, depth, enss, lats, lons, cycle_block.shape[0],
        1.0 / math.sqrt(cell_count),
    )
    vmem = pl.BlockSpec(memory_space=pltpu.VMEM)
    hbm = pl.BlockSpec(memory_space=pltpu.HBM)
    smem = pl.BlockSpec(memory_space=pltpu.SMEM)
    cells = (members, own, chan)
    padded = (members, depth, chan)
    slots = 6 + 2 * members
    pushes = plane + lons - 1 + enss * lats - 1
    res, ing, weight_grad = pl.pallas_call(
        functools.partial(block_kernel, dims),
        out_shape=[
            pltpu.VMEM(cells, BF),
            pltpu.VMEM(cells, BF),
            pltpu.VMEM((basis, held, chan), F32),
        ],
        in_specs=[hbm] * 4 + [smem, smem] + [hbm] * 3,
        out_specs=[vmem] * 3,
        scratch_shapes=[
            pltpu.VMEM(padded, BF),
            pltpu.VMEM(padded, BF),
            pltpu.VMEM(cells, BF),
            pltpu.VMEM((basis, chan, chan), BF),
            pltpu.VMEM((members * own, basis * chan), BF),
            pltpu.VMEM((basis * own, depth), BF),
            pltpu.VMEM((basis * own, depth), BF),
            pltpu.VMEM((2, members * select.shape[0], chan), BF),
            pltpu.VMEM((2, 4, members * H, chan), BF),
            pltpu.VMEM((chunks, 2, lons, span, half), BF),
            pltpu.VMEM((chunks, lons, span, half), BF),
            pltpu.VMEM((chunks, plane - 1, lons, piece, half), BF),
            pltpu.VMEM((chunks, lons, piece, half), BF),
            pltpu.VMEM((chunks, lons - 1, piece, half), BF),
            pltpu.VMEM((chunks, 2, span, half), BF),
            pltpu.VMEM((lons - 1, span, half), BF),
            pltpu.VMEM((span, half), BF),
            pltpu.VMEM((basis * tall, reach * blocks), F32),
            pltpu.VMEM((basis, reach, blocks, taps), F32),
            pltpu.VMEM(pos.shape, jnp.int32),
            pltpu.VMEM(select.shape, BF),
            pltpu.VMEM(regroup.shape, BF),
            pltpu.SemaphoreType.DMA((10,)),
            pltpu.SemaphoreType.DMA((2, slots)),
            pltpu.SemaphoreType.DMA((2, slots)),
            pltpu.SemaphoreType.DMA((chunks, pushes)),
            pltpu.SemaphoreType.DMA((chunks, pushes)),
        ],
        compiler_params=pltpu.CompilerParams(
            collective_id=0, has_side_effects=True, vmem_limit_bytes=VMEM
        ),
    )(
        members_in.reshape(cells), out_grad.reshape(cells), weight,
        jnp.transpose(basis_blocks, (1, 2, 0, 3)), cycle_block, half_width.T,
        jnp.asarray(pos), jnp.asarray(select, dtype=BF), jnp.asarray(regroup, dtype=BF),
    )
    held_back = [res, ing, weight_grad]
    res, ing, weight_grad = pl.pallas_call(
        place_kernel,
        out_shape=[jax.ShapeDtypeStruct(a.shape, a.dtype) for a in held_back],
        in_specs=[vmem] * 3,
        out_specs=[hbm] * 3,
        scratch_shapes=[pltpu.SemaphoreType.DMA((sum(a.shape[0] for a in held_back),))],
        compiler_params=pltpu.CompilerParams(vmem_limit_bytes=VMEM // 4),
    )(*held_back)
    return (res.reshape(members_in.shape), ing.reshape(members_in.shape), weight_grad)


def solution(mesh):
    cells = P("ens", "lat", "lon", None)
    return jax.shard_map(
        shards,
        mesh=mesh,
        in_specs=(cells, cells, P(), P(), P(), P()),
        out_specs=(cells, cells, P(None, "lon", None)),
        check_vma=False,
    )
```
